32 devices in a mesh: groups: 2 (over y), wide: 4 (over z), narrow: 2 (over x), rep: 2 (over core).
Axes of the slice: x: 2, y: 2, z: 4, core: 2. Of those that a mesh axis runs over, the one named last changes fastest.
Arguments:
- state: bfloat16 [32, 2, 192, 4, 192], P(('groups', 'wide'), None, 'narrow', None, 'rep'), parts along dimension 0, may hold values from -8 to 8
- left_env: bfloat16 [32, 24, 192, 192], P(('groups', 'wide'), None, 'narrow'), parts along dimension 0, may hold values from -1 to 2
- right_env: bfloat16 [32, 24, 192, 192], P(('groups', 'wide'), None, 'rep'), parts along dimension 0, may hold values from -1 to 2
- mpo_tensor: float32 [24, 24, 2, 2], replicated, may hold values from -3 to 3
- sector_units: int32 [32], P('groups'), parts along dimension 0, may hold values from 1 to 6, 32 in all
- chosen: int32 [32], P('groups'), parts along dimension 0, may hold values from 0 to 1, as said below
Outputs:
- next_state: bfloat16 [32, 2, 192, 4, 192], P(('groups', 'wide'), None, 'narrow', None, 'rep'), parts along dimension 0
- lanczos_alpha: float32 [8], P('groups'), parts along dimension 0
- lanczos_beta: float32 [8], P('groups'), parts along dimension 0
The draws below stay inside these ranges and needn't reach their ends.
There are 2 independent parts, one for each index of `groups`. The reference program is written for one: setup_inputs(seed, part) draws one part's arguments, and reference() takes and returns one part's arrays. A program takes and returns all parts, laid end to end along the dimension named above; an argument that names none is the same for every part. Nothing has to cross between parts.
Inputs may be any that keep to these rules, and one draw needn't show every extreme that they name: Sector q holds 32 * sector_units[q] bond states; the entries sum to 32. `chosen`: at least one sector is marked.
All inputs are finite; a program needn't handle non-finite values.
Results may differ from the reference program's by a relative error of at most 0.0059.
Values may be sent and summed in bfloat16 or wider, within the bound.
A program may use at most 256 MiB of HBM per device.

```python
import math
import jax
import jax.numpy as jnp
import numpy as np
from jax import lax

UNIT = 32
MEAN_U = 2
MOST_U = 6
NV = 4
CHAN = 24
PHYS = 2
NQ = 16
CAP = 192


def draw_state(key, part):
    key = jax.random.fold_in(key, 11)
    first_key, second_key = jax.random.split(key)
    full_shape = (NQ, PHYS, CAP, NV, CAP)
    noise_part = jnp.clip(jax.random.normal(first_key, full_shape, jnp.float32), -4.0, 4.0)
    scales = jnp.exp(jax.random.uniform(second_key, (NQ, 1, 1, NV, 1), jnp.float32, math.log(0.5), math.log(2.0)))
    return (noise_part * scales).astype(jnp.bfloat16)


def with_identity(noise_part):
    rows_at = jnp.arange(CAP)[:, None]
    cols_at = jnp.arange(CAP)[None, :]
    diagonal = (rows_at == cols_at).astype(jnp.float32)
    channel_ids = jnp.arange(CHAN)
    carries = ((channel_ids == 0) | (channel_ids == 1)).astype(jnp.float32)
    identity = carries[None, :, None, None] * diagonal[None, None, :, :]
    return (noise_part / math.sqrt(2.0 * UNIT) + identity).astype(jnp.bfloat16)


def draw_left_env(key, part):
    key = jax.random.fold_in(key, 23)
    full_shape = (NQ, CHAN, CAP, CAP)
    noise_part = jnp.clip(jax.random.normal(key, full_shape, jnp.float32), -3.0, 3.0)
    return with_identity(noise_part)


def draw_right_env(key, part):
    key = jax.random.fold_in(key, 29)
    full_shape = (NQ, CHAN, CAP, CAP)
    noise_part = jnp.clip(jax.random.normal(key, full_shape, jnp.float32), -3.0, 3.0)
    return with_identity(noise_part)


def draw_chosen(key, part):
    key = jax.random.fold_in(key, 37)
    first_key, second_key = jax.random.split(key)
    coin_flips = jax.random.randint(first_key, (NQ,), 0, 2, jnp.int32)
    forced = jax.random.randint(second_key, (), 0, NQ, jnp.int32)
    marked = (jnp.arange(NQ, dtype=jnp.int32) == forced).astype(jnp.int32)
    return jnp.maximum(coin_flips, marked).astype(jnp.int32)


def split_up(amount, total, bound, lean):
    weights = [(1 << 20) // math.isqrt(grade ** lean) + 1 for grade in range(2, amount + 1)]
    spare, holding = total - bound - (amount - 1), [1] * (amount - 1)
    while spare > 0:
        candidates = [i for i in range(amount - 1) if holding[i] < bound]
        pool, budget = sum([weights[i] for i in candidates]), spare
        for i in candidates:
            more = min(bound - holding[i], max(1, budget * weights[i] // pool), spare)
            holding[i] = holding[i] + more
            spare = spare - more
    return np.array([bound] + holding)


def uneven_parts(own_key, number_of, total, limit, slope):
    if number_of == 2:
        one = jax.random.randint(own_key, (), max(1, total - limit), min(limit, total - 1) + 1)
        return jnp.stack([one, total - one])
    tallies = jnp.asarray(split_up(number_of, total, limit, slope), jnp.int32)
    twos = (number_of - 1) // 2
    giver, receiver = tallies[1:1 + 2 * twos:2], tallies[2:2 + 2 * twos:2]
    margin = jnp.minimum(giver - 1, limit - receiver)
    passed = jax.random.randint(jax.random.fold_in(own_key, 1), (twos,), 0, 1 << 20) % (margin + 1)
    tallies = tallies.at[1:1 + 2 * twos:2].set(giver - passed).at[2:2 + 2 * twos:2].set(receiver + passed)
    return tallies[jax.random.permutation(jax.random.fold_in(own_key, 2), number_of)]


def bell_draw(own_key, shape, scale, most, kind=jnp.bfloat16):
    values = scale * jax.random.normal(own_key, shape, jnp.float32)
    return jnp.clip(values, min=-most, max=most).astype(kind)


def setup_inputs(seed: int = 0, part: int = 0) -> dict:
    key_list = jax.random.split(jax.random.key(seed), 7)
    part_splits = jax.random.split(jax.random.fold_in(key_list[6], part), 7)
    return {
        "state": draw_state(jax.random.fold_in(jax.random.fold_in(key_list[6], part), 71), part),
        "left_env": draw_left_env(jax.random.fold_in(jax.random.fold_in(key_list[6], part), 71), part),
        "right_env": draw_right_env(jax.random.fold_in(jax.random.fold_in(key_list[6], part), 71), part),
        "mpo_tensor": bell_draw(key_list[3], (CHAN, CHAN, PHYS, PHYS), 0.5, 3.0, jnp.float32),
        "sector_units": uneven_parts(part_splits[4], NQ, MEAN_U * NQ, MOST_U, 2).astype(jnp.int32),
        "chosen": draw_chosen(jax.random.fold_in(jax.random.fold_in(key_list[6], part), 71), part),
    }


channel_charge = (0,) * 10 + (1,) * 7 + (-1,) * 7
small_term = 1e-06

def charge_rule(mpo_tensor):
    charges = jnp.array(channel_charge, jnp.int32)
    spin_ids = jnp.arange(PHYS, dtype=jnp.int32)
    spin_change = spin_ids[None, None, :, None] - spin_ids[None, None, None, :]
    wanted = charges[None, :, None, None] - charges[:, None, None, None]
    return jnp.where(spin_change == wanted, mpo_tensor, jnp.zeros_like(mpo_tensor))

def reference(state, left_env, right_env, mpo_tensor, sector_units, chosen):
    live_sizes = jnp.concatenate([sector_units, jnp.zeros((1,), jnp.int32)]) * UNIT
    positions = jnp.arange(CAP, dtype=jnp.int32)
    row_live = positions[None, :] < live_sizes[:NQ, None]
    col_sizes = jnp.stack([live_sizes[:NQ], live_sizes[1:]], 1)
    col_live = positions[None, None, :] < col_sizes[:, :, None]
    live_cells = row_live[:, None, :, None, None] & col_live[:, :, None, None, :]
    masked = jnp.where(live_cells, state, jnp.zeros_like(state))
    zero_sector = jnp.zeros((1,) + state.shape[1:], jnp.bfloat16)
    padded = jnp.concatenate([zero_sector, masked, zero_sector], 0)
    right_padded = jnp.concatenate([right_env, jnp.zeros((1,) + right_env.shape[1:], jnp.bfloat16)], 0)
    allowed = charge_rule(mpo_tensor)
    charges = jnp.array(channel_charge, jnp.int32)
    highest = lax.Precision.HIGHEST

    def one_sector(index):
        sources = padded[index + 1 - charges].astype(jnp.float32)
        left_block = left_env[index].astype(jnp.float32)
        mixed_left = jnp.einsum('wia,wsavb->wsivb', left_block, sources, precision=highest).astype(jnp.bfloat16)
        combined = jnp.einsum('wxts,wsivb->txivb', allowed, mixed_left.astype(jnp.float32), precision=highest).astype(jnp.bfloat16)
        right_block = jnp.stack([right_padded[index], right_padded[index + 1]], 0).astype(jnp.float32)
        return jnp.einsum('txivb,txbc->tivc', combined.astype(jnp.float32), right_block, precision=highest)
    applied = lax.map(one_sector, jnp.arange(NQ, dtype=jnp.int32))
    keep_cells = live_cells & (chosen[:, None, None, None, None] > 0)
    applied = jnp.where(keep_cells, applied, 0.0)
    restricted = jnp.where(keep_cells, masked.astype(jnp.float32), 0.0)
    summed_axes = (0, 1, 2, 4)
    weight = lax.optimization_barrier(jnp.sum(restricted * restricted, axis=summed_axes))
    correlation = lax.optimization_barrier(jnp.sum(restricted * applied, axis=summed_axes))
    lanczos_alpha = correlation / weight
    residual = applied - lanczos_alpha[None, None, None, :, None] * restricted
    lanczos_beta = jnp.sqrt((lax.optimization_barrier(jnp.sum(residual * residual, axis=summed_axes)) + small_term) / weight)
    next_state = (residual / lanczos_beta[None, None, None, :, None]).astype(jnp.bfloat16)
    return (next_state, lanczos_alpha, lanczos_beta)
```

```python
import functools
import jax
import jax.numpy as jnp
from jax import lax
from jax.experimental import pallas as pl
from jax.experimental.pallas import tpu as pltpu
from jax.sharding import PartitionSpec as P

UNIT = 32
PHYS = 2
LANES = 128
GROUP = 16
MESH = pl.DeviceIdType.MESH

small_term = 1e-06
channel_slices = {0: (0, 10), 1: (10, 17), -1: (17, 24)}
channel_count = 24
blocks = {
    0: ((0, 0, 0), (1, 1, 0), (1, 0, 1), (0, 1, -1)),
    1: ((0, 0, 1), (1, 1, 1), (0, 1, 0)),
    -1: ((0, 0, -1), (1, 1, -1), (1, 0, 0)),
}


def width(charge):
    low, high = channel_slices[charge]
    return high - low


def block_table():
    table, at = {}, 0
    for e, entries in blocks.items():
        for t, s, x in entries:
            table[(e, t, s, x)] = at
            at += width(x)
    return table, at


offsets, block_total = block_table()


def shifted(value, axis, steps):
    count = lax.axis_size(axis)
    initial, last = (max(0, -steps), min(count, count - steps))
    return lax.ppermute(value, axis, [(source, source + steps) for source in range(initial, last)])


def spread_rule(mpo_tensor, e):
    low, high = channel_slices[e]
    parts = []
    for t, s, x in blocks[e]:
        x_low, x_high = channel_slices[x]
        parts.append(mpo_tensor[low:high, x_low:x_high, t, s].T)
    exact = jnp.concatenate(parts, 0)
    coarse = lax.reduce_precision(exact, 8, 7)
    mixing = jnp.concatenate([coarse, exact - coarse], 1).astype(jnp.bfloat16)
    same = jnp.eye(GROUP, dtype=jnp.bfloat16)
    full = mixing[:, None, :, None] * same[None, :, None, :]
    return full.reshape(mixing.shape[0] * GROUP, mixing.shape[1] * GROUP)


def gather_kernel(state_ref, out_ref, local_sem, send_sem, recv_sem):
    nz, nx = lax.axis_size("wide"), lax.axis_size("narrow")
    z, x = lax.axis_index("wide"), lax.axis_index("narrow")
    owned, _, rows, _ = state_ref.shape
    mine = pl.ds(pl.multiple_of(x * rows, GROUP), rows)

    def other(dx):
        return lax.rem(x + dx, nx)

    barrier = pltpu.get_barrier_semaphore()
    for dx in range(nx):
        if dx:
            pl.semaphore_signal(
                barrier, inc=1, device_id={"narrow": other(dx)}, device_id_type=MESH
            )

        @pl.when(z < nz - 1)
        def _():
            pl.semaphore_signal(
                barrier,
                inc=1,
                device_id={"wide": z + 1, "narrow": other(dx)},
                device_id_type=MESH,
            )

        @pl.when(z > 0)
        def _():
            pl.semaphore_signal(
                barrier,
                inc=1,
                device_id={"wide": z - 1, "narrow": other(dx)},
                device_id_type=MESH,
            )

    sides = jnp.where(z > 0, 1, 0) + jnp.where(z < nz - 1, 1, 0)
    pl.semaphore_wait(barrier, nx * (1 + sides) - 1)

    def copy(kind, dx, step, source, target):
        return pltpu.make_async_remote_copy(
            src_ref=source,
            dst_ref=target,
            send_sem=send_sem.at[kind, dx],
            recv_sem=recv_sem.at[kind, dx],
            device_id={"wide": z + step, "narrow": other(dx)},
            device_id_type=MESH,
        )

    ups = [
        copy(0, dx, 1, state_ref.at[owned - 1], out_ref.at[0, :, mine]) for dx in range(nx)
    ]
    downs = [copy(1, dx, -1, state_ref.at[0], out_ref.at[owned + 1, :, mine]) for dx in range(nx)]
    across = [
        copy(2, dx, 0, state_ref, out_ref.at[pl.ds(1, owned), :, mine]) for dx in range(1, nx)
    ]
    keep = pltpu.make_async_copy(state_ref, out_ref.at[pl.ds(1, owned), :, mine], local_sem)

    @pl.when(z < nz - 1)
    def _():
        for one in ups[::-1]:
            one.start()

    @pl.when(z > 0)
    def _():
        for one in downs[::-1]:
            one.start()

    for one in across:
        one.start()
    keep.start()
    keep.wait()
    for one in across:
        one.wait_send()
        one.wait_recv()

    @pl.when(z < nz - 1)
    def _():
        for one in ups:
            one.wait_send()
        for one in downs:
            one.wait_recv()

    @pl.when(z > 0)
    def _():
        for one in downs:
            one.wait_send()
        for one in ups:
            one.wait_recv()


def gathered(state):
    owned, phys, rows, cells = state.shape
    nx = lax.axis_size("narrow")
    return pl.pallas_call(
        gather_kernel,
        out_shape=jax.ShapeDtypeStruct((owned + 2, phys, rows * nx, cells), state.dtype),
        in_specs=[pl.BlockSpec(memory_space=pl.ANY)],
        out_specs=pl.BlockSpec(memory_space=pl.ANY),
        scratch_shapes=[
            pltpu.SemaphoreType.DMA,
            pltpu.SemaphoreType.DMA((3, nx)),
            pltpu.SemaphoreType.DMA((3, nx)),
        ],
        compiler_params=pltpu.CompilerParams(collective_id=0, has_side_effects=True),
        name="gather_state",
    )(state)


def apply_kernel(
    first,
    count,
    vectors,
    info,
    source,
    left,
    right_same,
    right_next,
    mix_zero,
    mix_up,
    mix_down,
    out,
    kept,
    padded,
    mixed,
    combined,
    right,
):
    step = pl.program_id(0)
    rows, bond = left.shape[2], left.shape[3]
    cols = right_same.shape[2]
    chunk = 32 if rows % 32 == 0 else GROUP
    slots = padded.shape[0]
    slot = step + 1
    base = slots + 1
    row_start, col_start = info[base], info[base + 1]
    chosen = info[base + 2 + step]
    mixers = {0: mix_zero, 1: mix_up, -1: mix_down}

    @pl.when(step == 0)
    def _():
        right[:, cols:, :] = jnp.zeros((channel_count, LANES - cols, bond), right.dtype)
        row_ids = lax.broadcasted_iota(jnp.int32, (bond, cols), 0)
        col_ids = lax.broadcasted_iota(jnp.int32, (bond, cols), 1) + col_start

        def fill(j, carry):
            for s in range(PHYS):
                live = (row_ids < info[j]) & (col_ids < info[j + s])
                for v in range(vectors):
                    part = source[j, s, :, v * cols : (v + 1) * cols].astype(jnp.float32)
                    part = jnp.where(live, part, 0.0).astype(padded.dtype)
                    padded[j, s, :, v * LANES : v * LANES + cols] = part
                    padded[j, s, :, v * LANES + cols : (v + 1) * LANES] = jnp.zeros(
                        (bond, LANES - cols), padded.dtype
                    )
            return carry

        lax.fori_loop(0, slots, fill, 0)

    live_rows = jnp.clip(info[slot] - row_start, 0, rows) * jnp.where(chosen > 0, 1, 0)

    @pl.when(live_rows == 0)
    def _():
        out[...] = jnp.zeros(out.shape, out.dtype)
        kept[...] = jnp.zeros(kept.shape, kept.dtype)

    @pl.when(live_rows > 0)
    def _():
        own_rows = pl.ds(pl.multiple_of(row_start, GROUP), rows)
        for s in range(PHYS):
            for v in range(vectors):
                kept[0, s, v] = padded[slot, s, own_rows, v * LANES : v * LANES + cols]

        def mix(g, carry):
            here = pl.ds(pl.multiple_of(g * GROUP, GROUP), GROUP)
            for e, (low, high) in channel_slices.items():
                block = left[0, low:high, here, :].reshape((high - low) * GROUP, bond)
                block = jnp.concatenate([block, block], 0)
                total = jnp.dot(mixers[e][...], block, preferred_element_type=jnp.float32)
                at = offsets[(e,) + blocks[e][0]]
                n = mixers[e].shape[0] // GROUP
                mixed[at : at + n, here, :] = total.astype(mixed.dtype).reshape(n, GROUP, bond)
            return carry

        lax.fori_loop(0, live_rows // GROUP, mix, 0)
        chunks = live_rows // chunk

        for t in range(PHYS):
            right[:, :cols, :] = (right_same if t == 0 else right_next)[0]

            def combine(r, carry):
                here = pl.ds(pl.multiple_of(r * chunk, chunk), chunk)
                for x, (low, high) in channel_slices.items():
                    n, total = high - low, None
                    for (e, tt, s, xx), at in offsets.items():
                        if (tt, xx) != (t, x):
                            continue
                        rows_of = mixed[at : at + n, here, :].reshape(n * chunk, bond)
                        term = jnp.dot(
                            rows_of, padded[slot - e, s], preferred_element_type=jnp.float32
                        )
                        total = term if total is None else total + term
                    total = total.astype(combined.dtype)
                    for i in range(n):
                        for v in range(vectors):
                            combined[v, here, (low + i) * LANES : (low + i + 1) * LANES] = total[
                                i * chunk : (i + 1) * chunk, v * LANES : (v + 1) * LANES
                            ]
                return carry

            lax.fori_loop(0, chunks, combine, 0)
            for n in range(1, rows // chunk + 1):

                @pl.when(chunks == n)
                def _(n=n):
                    m = n * chunk
                    total = jnp.dot(
                        combined[:, :m, :].reshape(vectors * m, channel_count * LANES),
                        right[...].reshape(channel_count * LANES, bond),
                        preferred_element_type=jnp.float32,
                    )
                    for h in range(bond // cols):
                        ids = lax.broadcasted_iota(jnp.int32, (m, cols), 1) + h * cols
                        live = ids < info[slot + t]
                        for v in range(vectors):
                            piece = total[v * m : (v + 1) * m, h * cols : (h + 1) * cols]
                            out[h, 0, t, v, :m, :] = jnp.where(live, piece, 0.0)
                            if m < rows:
                                out[h, 0, t, v, m:, :] = jnp.zeros((rows - m, cols), out.dtype)


def applied_parts(info, source, left_env, right_same, right_at, right_next, next_at, mixers, first, count, vectors):
    slots, phys, bond, cells = source.shape
    rows, cols = left_env.shape[2], right_same.shape[2]
    halves = bond // cols

    def whole(array):
        return pl.BlockSpec(array.shape, lambda q, info: (0,) * array.ndim)

    window = slots
    grid_spec = pltpu.PrefetchScalarGridSpec(
        num_scalar_prefetch=1,
        grid=(count,),
        in_specs=[
            whole(source),
            pl.BlockSpec((1, channel_count, rows, bond), lambda q, info: (q + first, 0, 0, 0)),
            pl.BlockSpec((1, channel_count, cols, bond), lambda q, info: (q + right_at, 0, 0, 0)),
            pl.BlockSpec((1, channel_count, cols, bond), lambda q, info: (q + next_at, 0, 0, 0)),
        ]
        + [whole(m) for m in mixers],
        out_specs=[
            pl.BlockSpec((halves, 1, phys, vectors, rows, cols), lambda q, info: (0, q, 0, 0, 0, 0)),
            pl.BlockSpec((1, phys, vectors, rows, cols), lambda q, info: (q, 0, 0, 0, 0)),
        ],
        scratch_shapes=[
            pltpu.VMEM((window, phys, bond, vectors * LANES), jnp.bfloat16),
            pltpu.VMEM((block_total, rows, bond), jnp.bfloat16),
            pltpu.VMEM((vectors, rows, channel_count * LANES), jnp.bfloat16),
            pltpu.VMEM((channel_count, LANES, bond), jnp.bfloat16),
        ],
    )
    return pl.pallas_call(
        functools.partial(apply_kernel, first, count, vectors),
        grid_spec=grid_spec,
        out_shape=[
            jax.ShapeDtypeStruct((halves, count, phys, vectors, rows, cols), jnp.float32),
            jax.ShapeDtypeStruct((count, phys, vectors, rows, cols), jnp.bfloat16),
        ],
        compiler_params=pltpu.CompilerParams(
            vmem_limit_bytes=56 * 1024 * 1024, dimension_semantics=("arbitrary",)
        ),
        cost_estimate=pl.CostEstimate(
            flops=20 * 10**9 * count // 4, bytes_accessed=12 * 10**6, transcendentals=0
        ),
        name="apply_sectors",
    )(info, source, left_env, right_same, right_next, *mixers)


def ratio(top, bottom):
    return jnp.where(bottom > 0, top / jnp.where(bottom > 0, bottom, 1.0), 0.0)


def merged(slots):
    weights = [s[:, 0:1] for s in slots]
    correlations = [s[:, 1:2] for s in slots]
    squares = [s[:, 2:3] for s in slots]
    weight, correlation, squared = sum(weights), sum(correlations), sum(squares)
    center = ratio(correlation, weight)
    for w, c in zip(weights, correlations):
        shift = ratio(c, w) - center
        squared = squared + shift * shift * w
    return weight, correlation, squared


def as_tile(columns):
    lane = lax.broadcasted_iota(jnp.int32, (8, LANES), 1)
    tile = jnp.zeros((8, LANES), jnp.float32)
    for i, column in enumerate(columns):
        tile = jnp.where(lane == i, column, tile)
    return tile


def finish_kernel(
    vectors, sums, kept, out, scalars, arrived, near, far, send_sem, recv_sem, near_send, near_recv, far_send, far_recv
):
    nz, nx, nc = lax.axis_size("wide"), lax.axis_size("narrow"), lax.axis_size("rep")
    z, x, c = lax.axis_index("wide"), lax.axis_index("narrow"), lax.axis_index("rep")
    total = nx * nc
    place = x * nc + c
    blocks_here = arrived.shape[0]

    def near_id(d):
        target = lax.rem(place + d, total)
        return {"narrow": target // nc, "rep": lax.rem(target, nc)}

    def far_id(d):
        return {"wide": lax.rem(z + d, nz)}

    barrier = pltpu.get_barrier_semaphore()
    for d in range(1, total):
        pl.semaphore_signal(barrier, inc=1, device_id=near_id(d), device_id_type=MESH)
    for d in range(1, nz):
        pl.semaphore_signal(barrier, inc=1, device_id=far_id(d), device_id_type=MESH)
    pl.semaphore_wait(barrier, total + nz - 2)

    exchange = pltpu.make_async_remote_copy(
        src_ref=sums.at[1 - c],
        dst_ref=arrived,
        send_sem=send_sem,
        recv_sem=recv_sem,
        device_id={"rep": 1 - c},
        device_id_type=MESH,
    )
    exchange.start()
    exchange.wait_recv()

    shape = arrived.shape[1:]
    lines = lax.broadcasted_iota(jnp.int32, (8, 1), 0)
    stats = [jnp.zeros((8, 1), jnp.float32) for _ in range(3)]
    for v in range(vectors):
        zero = jnp.zeros(shape, jnp.float32)

        def first_pass(i, carry):
            at = i * vectors + v
            value = arrived[at] + sums[c, at]
            arrived[at] = value
            state = kept[at].astype(jnp.float32)
            return (carry[0] + state * state, carry[1] + state * value)

        weight, correlation = lax.fori_loop(0, blocks_here // vectors, first_pass, (zero, zero))
        weight = jnp.sum(weight, keepdims=True)
        correlation = jnp.sum(correlation, keepdims=True)
        center = ratio(correlation, weight)

        def second_pass(i, carry):
            at = i * vectors + v
            rest = arrived[at] - center * kept[at].astype(jnp.float32)
            return carry + rest * rest

        squared = lax.fori_loop(0, blocks_here // vectors, second_pass, zero)
        squared = jnp.sum(squared, keepdims=True)
        for i, value in enumerate((weight, correlation, squared)):
            stats[i] = jnp.where(lines == v, value, stats[i])

    near[place] = as_tile(stats)
    copies = [
        pltpu.make_async_remote_copy(
            src_ref=near.at[place],
            dst_ref=near.at[place],
            send_sem=near_send.at[d],
            recv_sem=near_recv.at[d],
            device_id=near_id(d),
            device_id_type=MESH,
        )
        for d in range(1, total)
    ]
    for one in copies:
        one.start()
    for one in copies:
        one.wait_recv()
    far[z] = as_tile(merged([near[i] for i in range(total)]))
    far_copies = [
        pltpu.make_async_remote_copy(
            src_ref=far.at[z],
            dst_ref=far.at[z],
            send_sem=far_send.at[d],
            recv_sem=far_recv.at[d],
            device_id=far_id(d),
            device_id_type=MESH,
        )
        for d in range(1, nz)
    ]
    for one in far_copies:
        one.start()
    for one in far_copies:
        one.wait_recv()
    weight, correlation, squared = merged([far[i] for i in range(nz)])
    alpha = correlation / weight
    beta = jnp.sqrt((squared + small_term) / weight)
    scalars[...] = as_tile((alpha, beta))
    for v in range(vectors):
        own_alpha, own_beta = alpha[v : v + 1], beta[v : v + 1]

        def last_pass(i, carry):
            at = i * vectors + v
            rest = arrived[at] - own_alpha * kept[at].astype(jnp.float32)
            out[at] = (rest / own_beta).astype(out.dtype)
            return carry

        lax.fori_loop(0, blocks_here // vectors, last_pass, 0)
    exchange.wait_send()
    for one in copies + far_copies:
        one.wait_send()


def finished(sums, kept, vectors):
    halves, blocks_here, rows, cols = sums.shape
    near_count = lax.axis_size("narrow") * lax.axis_size("rep")
    far_count = lax.axis_size("wide")
    vmem = pl.BlockSpec(memory_space=pltpu.VMEM)
    dma = pltpu.SemaphoreType.DMA
    return pl.pallas_call(
        functools.partial(finish_kernel, vectors),
        out_shape=[
            jax.ShapeDtypeStruct((blocks_here, rows, cols), jnp.bfloat16),
            jax.ShapeDtypeStruct((8, LANES), jnp.float32),
        ],
        in_specs=[vmem] * 2,
        out_specs=[vmem] * 2,
        scratch_shapes=[
            pltpu.VMEM((blocks_here, rows, cols), jnp.float32),
            pltpu.VMEM((near_count, 8, LANES), jnp.float32),
            pltpu.VMEM((far_count, 8, LANES), jnp.float32),
            dma,
            dma,
            dma((near_count,)),
            dma((near_count,)),
            dma((far_count,)),
            dma((far_count,)),
        ],
        compiler_params=pltpu.CompilerParams(
            collective_id=1, has_side_effects=True, vmem_limit_bytes=48 * 1024 * 1024
        ),
        name="finish_step",
    )(sums, kept)


def body(state, left_env, right_env, mpo_tensor, sector_units, chosen):
    owned, phys, rows, vectors, cols = state.shape
    first_sector = lax.axis_index("wide") * owned
    row_start = lax.axis_index("narrow") * rows
    col_start = lax.axis_index("rep") * cols
    following = shifted(right_env[:1], "wide", -1)
    none = jnp.zeros((1,), jnp.int32)
    sizes = jnp.concatenate([none, sector_units * UNIT, none, none])
    info = jnp.concatenate(
        [
            lax.dynamic_slice_in_dim(sizes, first_sector, owned + 3),
            row_start[None],
            col_start[None],
            lax.dynamic_slice_in_dim(chosen, first_sector, owned),
        ]
    ).astype(jnp.int32)
    mixers = [spread_rule(mpo_tensor, e) for e in channel_slices]
    source = gathered(state.reshape(owned, phys, rows, vectors * cols))
    raised = jnp.concatenate([right_env[1:], following], 0)
    sums, kept = applied_parts(
        info, source, left_env, right_env, 0, raised, 0, mixers, 0, owned, vectors
    )
    shape = (owned * phys * vectors, rows, cols)
    out, scalars = finished(sums.reshape((sums.shape[0],) + shape), kept.reshape(shape), vectors)
    next_state = out.reshape(owned, phys, vectors, rows, cols).transpose(0, 1, 3, 2, 4)
    return (next_state, scalars[:vectors, 0], scalars[:vectors, 1])


def solution(mesh):
    placed = (
        P(("groups", "wide"), None, "narrow", None, "rep"),
        P(("groups", "wide"), None, "narrow", None),
        P(("groups", "wide"), None, "rep", None),
        P(),
        P("groups"),
        P("groups"),
    )
    return jax.shard_map(
        body,
        mesh=mesh,
        in_specs=placed,
        out_specs=(P(("groups", "wide"), None, "narrow", None, "rep"), P("groups"), P("groups")),
        check_vma=False,
    )
```

```python
import functools
import jax
import jax.numpy as jnp
from jax import lax
from jax.experimental import pallas as pl
from jax.experimental.pallas import tpu as pltpu
from jax.sharding import PartitionSpec as P

UNIT = 32
PHYS = 2
LANES = 128
GROUP = 16
MESH = pl.DeviceIdType.MESH

small_term = 1e-06
channel_slices = {0: (0, 10), 1: (10, 17), -1: (17, 24)}
channel_count = 24
blocks = {
    0: ((0, 0, 0), (1, 1, 0), (1, 0, 1), (0, 1, -1)),
    1: ((0, 0, 1), (1, 1, 1), (0, 1, 0)),
    -1: ((0, 0, -1), (1, 1, -1), (1, 0, 0)),
}


def width(charge):
    low, high = channel_slices[charge]
    return high - low


def block_table():
    table, at = {}, 0
    for e, entries in blocks.items():
        for t, s, x in entries:
            table[(e, t, s, x)] = at
            at += width(x)
    return table, at


offsets, block_total = block_table()


def shifted(value, axis, steps):
    count = lax.axis_size(axis)
    initial, last = (max(0, -steps), min(count, count - steps))
    return lax.ppermute(value, axis, [(source, source + steps) for source in range(initial, last)])


def spread(rule, mixers):
    for e, (low, high) in channel_slices.items():
        n, depth = high - low, 2 * (high - low) * GROUP
        at = 0
        for t, s, x in blocks[e]:
            x_low, x_high = channel_slices[x]
            m = x_high - x_low
            exact = rule[t, s, x_low:x_high, low:high]
            coarse = exact.astype(jnp.bfloat16)
            rest = (exact - coarse.astype(jnp.float32)).astype(jnp.bfloat16)
            row = lax.broadcasted_iota(jnp.int32, (m * GROUP, m), 0) // GROUP
            up = jnp.where(row == lax.broadcasted_iota(jnp.int32, (m * GROUP, m), 1), 1.0, 0.0)
            up = up.astype(jnp.bfloat16)
            col = lax.broadcasted_iota(jnp.int32, (n, depth), 1) // GROUP
            line = lax.broadcasted_iota(jnp.int32, (n, depth), 0)
            total = None
            for part, start in ((coarse, 0), (rest, n)):
                side = jnp.where(col == line + start, 1.0, 0.0).astype(jnp.bfloat16)
                tall = jnp.dot(up, part, preferred_element_type=jnp.float32).astype(jnp.bfloat16)
                term = jnp.dot(tall, side, preferred_element_type=jnp.float32)
                total = term if total is None else total + term
            shape = (m * GROUP, depth)
            same = lax.broadcasted_iota(jnp.int32, shape, 0) % GROUP == (
                lax.broadcasted_iota(jnp.int32, shape, 1) % GROUP
            )
            mixers[e][at : at + m * GROUP, :] = jnp.where(same, total, 0.0).astype(jnp.bfloat16)
            at += m * GROUP


def gather_kernel(state_ref, out_ref, local_sem, send_sem, recv_sem):
    nz, nx = lax.axis_size("wide"), lax.axis_size("narrow")
    z, x = lax.axis_index("wide"), lax.axis_index("narrow")
    owned, _, rows, _ = state_ref.shape
    mine = pl.ds(pl.multiple_of(x * rows, GROUP), rows)

    def other(dx):
        return lax.rem(x + dx, nx)

    barrier = pltpu.get_barrier_semaphore()
    for dx in range(nx):
        if dx:
            pl.semaphore_signal(
                barrier, inc=1, device_id={"narrow": other(dx)}, device_id_type=MESH
            )

        @pl.when(z < nz - 1)
        def _():
            pl.semaphore_signal(
                barrier,
                inc=1,
                device_id={"wide": z + 1, "narrow": other(dx)},
                device_id_type=MESH,
            )

        @pl.when(z > 0)
        def _():
            pl.semaphore_signal(
                barrier,
                inc=1,
                device_id={"wide": z - 1, "narrow": other(dx)},
                device_id_type=MESH,
            )

    sides = jnp.where(z > 0, 1, 0) + jnp.where(z < nz - 1, 1, 0)
    pl.semaphore_wait(barrier, nx * (1 + sides) - 1)

    def copy(kind, dx, step, source, target):
        return pltpu.make_async_remote_copy(
            src_ref=source,
            dst_ref=target,
            send_sem=send_sem.at[kind, dx],
            recv_sem=recv_sem.at[kind, dx],
            device_id={"wide": z + step, "narrow": other(dx)},
            device_id_type=MESH,
        )

    ups = [
        copy(0, dx, 1, state_ref.at[owned - 1], out_ref.at[0, :, mine]) for dx in range(nx)
    ]
    downs = [copy(1, dx, -1, state_ref.at[0], out_ref.at[owned + 1, :, mine]) for dx in range(nx)]
    across = [
        copy(2, dx, 0, state_ref, out_ref.at[pl.ds(1, owned), :, mine]) for dx in range(1, nx)
    ]
    keep = pltpu.make_async_copy(state_ref, out_ref.at[pl.ds(1, owned), :, mine], local_sem)

    @pl.when(z < nz - 1)
    def _():
        for one in ups[::-1]:
            one.start()

    @pl.when(z > 0)
    def _():
        for one in downs[::-1]:
            one.start()

    for one in across:
        one.start()
    keep.start()
    keep.wait()
    for one in across:
        one.wait_send()
        one.wait_recv()

    @pl.when(z < nz - 1)
    def _():
        for one in ups:
            one.wait_send()
        for one in downs:
            one.wait_recv()

    @pl.when(z > 0)
    def _():
        for one in downs:
            one.wait_send()
        for one in ups:
            one.wait_recv()


def gathered(state):
    owned, phys, rows, cells = state.shape
    nx = lax.axis_size("narrow")
    return pl.pallas_call(
        gather_kernel,
        out_shape=jax.ShapeDtypeStruct((owned + 2, phys, rows * nx, cells), state.dtype),
        in_specs=[pl.BlockSpec(memory_space=pl.ANY)],
        out_specs=pl.BlockSpec(memory_space=pl.ANY),
        scratch_shapes=[
            pltpu.SemaphoreType.DMA,
            pltpu.SemaphoreType.DMA((3, nx)),
            pltpu.SemaphoreType.DMA((3, nx)),
        ],
        compiler_params=pltpu.CompilerParams(collective_id=0, has_side_effects=True),
        name="gather_state",
    )(state)


def apply_kernel(
    count,
    vectors,
    info,
    source,
    left,
    right_same,
    right_next,
    right_last,
    rule,
    out,
    passed,
    kept,
    padded,
    mixed,
    combined,
    right,
    mix_zero,
    mix_up,
    mix_down,
):
    step = pl.program_id(0)
    rows, bond = left.shape[2], left.shape[3]
    cols = right_same.shape[2]
    chunk = 32 if rows % 32 == 0 else GROUP
    slots = padded.shape[0]
    slot = step + 1
    base = slots + 1
    row_start, col_start = info[base], info[base + 1]
    chosen = info[base + 2 + step]
    mixers = {0: mix_zero, 1: mix_up, -1: mix_down}

    @pl.when(step == 0)
    def _():
        spread(rule, mixers)
        right[:, cols:, :] = jnp.zeros((channel_count, LANES - cols, bond), right.dtype)
        row_ids = lax.broadcasted_iota(jnp.int32, (bond, cols), 0)
        col_ids = lax.broadcasted_iota(jnp.int32, (bond, cols), 1) + col_start

        def fill(j, carry):
            for s in range(PHYS):
                live = (row_ids < info[j]) & (col_ids < info[j + s])
                for v in range(vectors):
                    part = source[j, s, :, v * cols : (v + 1) * cols].astype(jnp.float32)
                    part = jnp.where(live, part, 0.0).astype(padded.dtype)
                    padded[j, s, :, v * LANES : v * LANES + cols] = part
                    padded[j, s, :, v * LANES + cols : (v + 1) * LANES] = jnp.zeros(
                        (bond, LANES - cols), padded.dtype
                    )
            return carry

        lax.fori_loop(0, slots, fill, 0)

    live_rows = jnp.clip(info[slot] - row_start, 0, rows) * jnp.where(chosen > 0, 1, 0)

    @pl.when(live_rows == 0)
    def _():
        out[...] = jnp.zeros(out.shape, out.dtype)
        passed[...] = jnp.zeros(passed.shape, passed.dtype)
        kept[...] = jnp.zeros(kept.shape, kept.dtype)

    @pl.when(live_rows > 0)
    def _():
        own_rows = pl.ds(pl.multiple_of(row_start, GROUP), rows)
        for s in range(PHYS):
            for v in range(vectors):
                kept[0, s, v] = padded[slot, s, own_rows, v * LANES : v * LANES + cols]

        def mix(g, carry):
            here = pl.ds(pl.multiple_of(g * GROUP, GROUP), GROUP)
            for e, (low, high) in channel_slices.items():
                block = left[0, low:high, here, :].reshape((high - low) * GROUP, bond)
                block = jnp.concatenate([block, block], 0)
                total = jnp.dot(mixers[e][...], block, preferred_element_type=jnp.float32)
                at = offsets[(e,) + blocks[e][0]]
                n = mixers[e].shape[0] // GROUP
                mixed[at : at + n, here, :] = total.astype(mixed.dtype).reshape(n, GROUP, bond)
            return carry

        lax.fori_loop(0, live_rows // GROUP, mix, 0)
        chunks = live_rows // chunk

        for t in range(PHYS):
            if t == 0:
                right[:, :cols, :] = right_same[0]
            else:

                @pl.when(step < count - 1)
                def _():
                    right[:, :cols, :] = right_next[0]

                @pl.when(step == count - 1)
                def _():
                    right[:, :cols, :] = right_last[0]

            def combine(r, carry):
                here = pl.ds(pl.multiple_of(r * chunk, chunk), chunk)
                for x, (low, high) in channel_slices.items():
                    n, total = high - low, None
                    for (e, tt, s, xx), at in offsets.items():
                        if (tt, xx) != (t, x):
                            continue
                        rows_of = mixed[at : at + n, here, :].reshape(n * chunk, bond)
                        term = jnp.dot(
                            rows_of, padded[slot - e, s], preferred_element_type=jnp.float32
                        )
                        total = term if total is None else total + term
                    total = total.astype(combined.dtype)
                    for i in range(n):
                        for v in range(vectors):
                            combined[v, here, (low + i) * LANES : (low + i + 1) * LANES] = total[
                                i * chunk : (i + 1) * chunk, v * LANES : (v + 1) * LANES
                            ]
                return carry

            lax.fori_loop(0, chunks, combine, 0)
            for n in range(1, rows // chunk + 1):

                @pl.when(chunks == n)
                def _(n=n):
                    m = n * chunk
                    total = jnp.dot(
                        combined[:, :m, :].reshape(vectors * m, channel_count * LANES),
                        right[...].reshape(channel_count * LANES, bond),
                        preferred_element_type=jnp.float32,
                    )
                    ids = lax.broadcasted_iota(jnp.int32, (m, cols), 1)
                    low_half = ids < info[slot + t]
                    high_half = ids + cols < info[slot + t]
                    for v in range(vectors):
                        piece = total[v * m : (v + 1) * m]
                        low_piece = jnp.where(low_half, piece[:, :cols], 0.0)
                        high_piece = jnp.where(high_half, piece[:, cols:], 0.0)
                        own = jnp.where(col_start == 0, low_piece, high_piece)
                        sent = jnp.where(col_start == 0, high_piece, low_piece)
                        out[0, t, v, :m, :] = own
                        passed[0, t, v, :m, :] = sent.astype(passed.dtype)
                        if m < rows:
                            rest = (rows - m, cols)
                            out[0, t, v, m:, :] = jnp.zeros(rest, out.dtype)
                            passed[0, t, v, m:, :] = jnp.zeros(rest, passed.dtype)


def applied_parts(info, source, left_env, right_env, right_last, rule, vectors):
    slots, phys, bond, cells = source.shape
    count = left_env.shape[0]
    rows, cols = left_env.shape[2], right_env.shape[2]

    def whole(array):
        return pl.BlockSpec(array.shape, lambda q, info: (0,) * array.ndim)

    def result(q, info):
        return (q, 0, 0, 0, 0)

    block = (1, phys, vectors, rows, cols)
    full = (count, phys, vectors, rows, cols)
    grid_spec = pltpu.PrefetchScalarGridSpec(
        num_scalar_prefetch=1,
        grid=(count,),
        in_specs=[
            whole(source),
            pl.BlockSpec((1, channel_count, rows, bond), lambda q, info: (q, 0, 0, 0)),
            pl.BlockSpec((1, channel_count, cols, bond), lambda q, info: (q, 0, 0, 0)),
            pl.BlockSpec(
                (1, channel_count, cols, bond),
                lambda q, info: (jnp.minimum(q + 1, count - 1), 0, 0, 0),
            ),
            whole(right_last),
            whole(rule),
        ],
        out_specs=[pl.BlockSpec(block, result) for _ in range(3)],
        scratch_shapes=[
            pltpu.VMEM((slots, phys, bond, vectors * LANES), jnp.bfloat16),
            pltpu.VMEM((block_total, rows, bond), jnp.bfloat16),
            pltpu.VMEM((vectors, rows, channel_count * LANES), jnp.bfloat16),
            pltpu.VMEM((channel_count, LANES, bond), jnp.bfloat16),
        ]
        + [
            pltpu.VMEM(
                (GROUP * sum(width(x) for _, _, x in blocks[e]), 2 * GROUP * width(e)),
                jnp.bfloat16,
            )
            for e in channel_slices
        ],
    )
    return pl.pallas_call(
        functools.partial(apply_kernel, count, vectors),
        grid_spec=grid_spec,
        out_shape=[
            jax.ShapeDtypeStruct(full, jnp.float32),
            jax.ShapeDtypeStruct(full, jnp.bfloat16),
            jax.ShapeDtypeStruct(full, jnp.bfloat16),
        ],
        compiler_params=pltpu.CompilerParams(
            vmem_limit_bytes=56 * 1024 * 1024, dimension_semantics=("arbitrary",)
        ),
        cost_estimate=pl.CostEstimate(
            flops=5 * 10**9 * count, bytes_accessed=12 * 10**6, transcendentals=0
        ),
        name="apply_sectors",
    )(info, source, left_env, right_env, right_env, right_last, rule)


def ratio(top, bottom):
    return jnp.where(bottom > 0, top / jnp.where(bottom > 0, bottom, 1.0), 0.0)


def merged(slots):
    weights = [s[:, 0:1] for s in slots]
    correlations = [s[:, 1:2] for s in slots]
    squares = [s[:, 2:3] for s in slots]
    weight, correlation, squared = sum(weights), sum(correlations), sum(squares)
    center = ratio(correlation, weight)
    for w, c in zip(weights, correlations):
        shift = ratio(c, w) - center
        squared = squared + shift * shift * w
    return weight, correlation, squared


def as_tile(columns):
    lane = lax.broadcasted_iota(jnp.int32, (8, LANES), 1)
    tile = jnp.zeros((8, LANES), jnp.float32)
    for i, column in enumerate(columns):
        tile = jnp.where(lane == i, column, tile)
    return tile


def finish_kernel(
    vectors,
    own_ref,
    passed,
    kept_ref,
    out,
    scalars,
    value_of,
    kept,
    arrived,
    totals,
    near,
    far,
    own_sem,
    kept_sem,
    send_sem,
    recv_sem,
    near_send,
    near_recv,
    far_send,
    far_recv,
):
    nz, nx, nc = lax.axis_size("wide"), lax.axis_size("narrow"), lax.axis_size("rep")
    z, x, c = lax.axis_index("wide"), lax.axis_index("narrow"), lax.axis_index("rep")
    total = nx * nc
    place = x * nc + c
    blocks_here = arrived.shape[0]
    pieces = send_sem.shape[0]
    per_piece = blocks_here // pieces
    loads = []
    for k in range(pieces):
        here = pl.ds(k * per_piece, per_piece)
        loads.append(
            (
                pltpu.make_async_copy(own_ref.at[here], value_of.at[here], own_sem.at[k]),
                pltpu.make_async_copy(kept_ref.at[here], kept.at[here], kept_sem.at[k]),
            )
        )
        for one in loads[-1]:
            one.start()

    def near_id(d):
        target = lax.rem(place + d, total)
        return {"narrow": target // nc, "rep": lax.rem(target, nc)}

    def far_id(d):
        return {"wide": lax.rem(z + d, nz)}

    barrier = pltpu.get_barrier_semaphore()
    for d in range(1, total):
        pl.semaphore_signal(barrier, inc=1, device_id=near_id(d), device_id_type=MESH)
    for d in range(1, nz):
        pl.semaphore_signal(barrier, inc=1, device_id=far_id(d), device_id_type=MESH)
    pl.semaphore_wait(barrier, total + nz - 2)

    exchanges = []
    for k in range(pieces):
        here = pl.ds(k * per_piece, per_piece)
        exchanges.append(
            pltpu.make_async_remote_copy(
                src_ref=passed.at[here],
                dst_ref=arrived.at[here],
                send_sem=send_sem.at[k],
                recv_sem=recv_sem.at[k],
                device_id={"rep": 1 - c},
                device_id_type=MESH,
            )
        )
        exchanges[-1].start()

    shape = arrived.shape[1:]
    totals[...] = jnp.zeros(totals.shape, jnp.float32)
    for k in range(pieces):
        for one in loads[k]:
            one.wait()
        exchanges[k].wait_recv()

        def first_pass(v, carry):
            weight, correlation = totals[0, v], totals[1, v]
            for i in range(per_piece // vectors):
                at = k * per_piece + i * vectors + v
                value = value_of[at] + arrived[at].astype(jnp.float32)
                value_of[at] = value
                state = kept[at].astype(jnp.float32)
                weight += state * state
                correlation += state * value
            totals[0, v] = weight
            totals[1, v] = correlation
            return carry

        lax.fori_loop(0, vectors, first_pass, 0)

    lines = lax.broadcasted_iota(jnp.int32, (8, 1), 0)
    stats = [jnp.zeros((8, 1), jnp.float32) for _ in range(3)]
    for v in range(vectors):
        zero = jnp.zeros(shape, jnp.float32)
        weight = jnp.sum(totals[0, v], keepdims=True)
        correlation = jnp.sum(totals[1, v], keepdims=True)
        center = ratio(correlation, weight)

        def second_pass(i, carry):
            at = i * vectors + v
            rest = value_of[at] - center * kept[at].astype(jnp.float32)
            return carry + rest * rest

        squared = lax.fori_loop(0, blocks_here // vectors, second_pass, zero)
        squared = jnp.sum(squared, keepdims=True)
        for i, value in enumerate((weight, correlation, squared)):
            stats[i] = jnp.where(lines == v, value, stats[i])

    near[place] = as_tile(stats)
    copies = [
        pltpu.make_async_remote_copy(
            src_ref=near.at[place],
            dst_ref=near.at[place],
            send_sem=near_send.at[d],
            recv_sem=near_recv.at[d],
            device_id=near_id(d),
            device_id_type=MESH,
        )
        for d in range(1, total)
    ]
    for one in copies:
        one.start()
    for one in copies:
        one.wait_recv()
    far[z] = as_tile(merged([near[i] for i in range(total)]))
    far_copies = [
        pltpu.make_async_remote_copy(
            src_ref=far.at[z],
            dst_ref=far.at[z],
            send_sem=far_send.at[d],
            recv_sem=far_recv.at[d],
            device_id=far_id(d),
            device_id_type=MESH,
        )
        for d in range(1, nz)
    ]
    for one in far_copies:
        one.start()
    for one in far_copies:
        one.wait_recv()
    weight, correlation, squared = merged([far[i] for i in range(nz)])
    alpha = correlation / weight
    beta = jnp.sqrt((squared + small_term) / weight)
    scalars[...] = as_tile((alpha, beta))
    for v in range(vectors):
        own_alpha, own_beta = alpha[v : v + 1], beta[v : v + 1]

        def last_pass(i, carry):
            at = i * vectors + v
            rest = value_of[at] - own_alpha * kept[at].astype(jnp.float32)
            out[at] = (rest / own_beta).astype(out.dtype)
            return carry

        lax.fori_loop(0, blocks_here // vectors, last_pass, 0)
    for one in exchanges + copies + far_copies:
        one.wait_send()


def finished(own, passed, kept, vectors):
    blocks_here, rows, cols = own.shape
    near_count = lax.axis_size("narrow") * lax.axis_size("rep")
    far_count = lax.axis_size("wide")
    pieces = blocks_here // (PHYS * vectors)
    dma = pltpu.SemaphoreType.DMA
    return pl.pallas_call(
        functools.partial(finish_kernel, vectors),
        out_shape=[
            jax.ShapeDtypeStruct((blocks_here, rows, cols), jnp.bfloat16),
            jax.ShapeDtypeStruct((8, LANES), jnp.float32),
        ],
        in_specs=[pl.BlockSpec(memory_space=pl.ANY)] * 3,
        out_specs=[pl.BlockSpec(memory_space=pltpu.VMEM)] * 2,
        scratch_shapes=[
            pltpu.VMEM((blocks_here, rows, cols), jnp.float32),
            pltpu.VMEM((blocks_here, rows, cols), jnp.bfloat16),
            pltpu.VMEM((blocks_here, rows, cols), jnp.bfloat16),
            pltpu.VMEM((2, vectors, rows, cols), jnp.float32),
            pltpu.VMEM((near_count, 8, LANES), jnp.float32),
            pltpu.VMEM((far_count, 8, LANES), jnp.float32),
            dma((pieces,)),
            dma((pieces,)),
            dma((pieces,)),
            dma((pieces,)),
            dma((near_count,)),
            dma((near_count,)),
            dma((far_count,)),
            dma((far_count,)),
        ],
        compiler_params=pltpu.CompilerParams(
            collective_id=1, has_side_effects=True, vmem_limit_bytes=48 * 1024 * 1024
        ),
        name="finish_step",
    )(own, passed, kept)


def body(state, left_env, right_env, mpo_tensor, sector_units, chosen):
    owned, phys, rows, vectors, cols = state.shape
    first_sector = lax.axis_index("wide") * owned
    row_start = lax.axis_index("narrow") * rows
    col_start = lax.axis_index("rep") * cols
    following = shifted(right_env[:1], "wide", -1)
    none = jnp.zeros((1,), jnp.int32)
    sizes = jnp.concatenate([none, sector_units * UNIT, none, none])
    info = jnp.concatenate(
        [
            lax.dynamic_slice_in_dim(sizes, first_sector, owned + 3),
            row_start[None],
            col_start[None],
            lax.dynamic_slice_in_dim(chosen, first_sector, owned),
        ]
    ).astype(jnp.int32)
    rule = jnp.transpose(mpo_tensor, (2, 3, 1, 0))
    source = gathered(state.reshape(owned, phys, rows, vectors * cols))
    parts = applied_parts(info, source, left_env, right_env, following, rule, vectors)
    out, scalars = finished(
        *(part.reshape(owned * phys * vectors, rows, cols) for part in parts), vectors
    )
    next_state = out.reshape(owned, phys, vectors, rows, cols).transpose(0, 1, 3, 2, 4)
    return (next_state, scalars[:vectors, 0], scalars[:vectors, 1])


def solution(mesh):
    placed = (
        P(("groups", "wide"), None, "narrow", None, "rep"),
        P(("groups", "wide"), None, "narrow", None),
        P(("groups", "wide"), None, "rep", None),
        P(),
        P("groups"),
        P("groups"),
    )
    return jax.shard_map(
        body,
        mesh=mesh,
        in_specs=placed,
        out_specs=(P(("groups", "wide"), None, "narrow", None, "rep"), P("groups"), P("groups")),
        check_vma=False,
    )
```

```python
import functools
import jax
import jax.numpy as jnp
from jax import lax
from jax.experimental import pallas as pl
from jax.experimental.pallas import tpu as pltpu
from jax.sharding import PartitionSpec as P

UNIT = 32
PHYS = 2
LANES = 128
GROUP = 16
MESH = pl.DeviceIdType.MESH

small_term = 1e-06
channel_slices = {0: (0, 10), 1: (10, 17), -1: (17, 24)}
channel_count = 24
blocks = {
    0: ((0, 0, 0), (1, 1, 0), (1, 0, 1), (0, 1, -1)),
    1: ((0, 0, 1), (1, 1, 1), (0, 1, 0)),
    -1: ((0, 0, -1), (1, 1, -1), (1, 0, 0)),
}


def width(charge):
    low, high = channel_slices[charge]
    return high - low


def block_table():
    table, at = {}, 0
    for e, entries in blocks.items():
        for t, s, x in entries:
            table[(e, t, s, x)] = at
            at += width(x)
    return table, at


offsets, block_total = block_table()


def packed_lanes(block):
    half = block.shape[0] // 2
    rest = block[:, :, LANES:]
    return jnp.concatenate(
        [block[:, :, :LANES], jnp.concatenate([rest[:half], rest[half:]], 2)], 0
    )


def spread(rule, mixers):
    for e, (low, high) in channel_slices.items():
        n, depth = high - low, 2 * (high - low) * GROUP
        at = 0
        for t, s, x in blocks[e]:
            x_low, x_high = channel_slices[x]
            m = x_high - x_low
            exact = rule[t, s, x_low:x_high, low:high]
            coarse = exact.astype(jnp.bfloat16)
            rest = (exact - coarse.astype(jnp.float32)).astype(jnp.bfloat16)
            row = lax.broadcasted_iota(jnp.int32, (m * GROUP, m), 0) // GROUP
            up = jnp.where(row == lax.broadcasted_iota(jnp.int32, (m * GROUP, m), 1), 1.0, 0.0)
            up = up.astype(jnp.bfloat16)
            col = lax.broadcasted_iota(jnp.int32, (n, depth), 1) // GROUP
            line = lax.broadcasted_iota(jnp.int32, (n, depth), 0)
            total = None
            for part, start in ((coarse, 0), (rest, n)):
                side = jnp.where(col == line + start, 1.0, 0.0).astype(jnp.bfloat16)
                tall = jnp.dot(up, part, preferred_element_type=jnp.float32).astype(jnp.bfloat16)
                term = jnp.dot(tall, side, preferred_element_type=jnp.float32)
                total = term if total is None else total + term
            shape = (m * GROUP, depth)
            same = lax.broadcasted_iota(jnp.int32, shape, 0) % GROUP == (
                lax.broadcasted_iota(jnp.int32, shape, 1) % GROUP
            )
            mixers[e][at : at + m * GROUP, :] = jnp.where(same, total, 0.0).astype(jnp.bfloat16)
            at += m * GROUP


def gather_kernel(
    state_ref,
    packed_ref,
    rule,
    out_ref,
    following_ref,
    mix_zero,
    mix_up,
    mix_down,
    local_sem,
    halo_send,
    halo_recv,
    cross_send,
    cross_recv,
    right_send,
    right_recv,
):
    nz, nx = lax.axis_size("wide"), lax.axis_size("narrow")
    z, x = lax.axis_index("wide"), lax.axis_index("narrow")
    owned, _, rows, _ = state_ref.shape
    mine = pl.ds(pl.multiple_of(x * rows, GROUP), rows)
    below, above = z > 0, z < nz - 1

    def other(dx):
        return lax.rem(x + dx, nx)

    barrier = pltpu.get_barrier_semaphore()
    for dx in range(1, nx):
        pl.semaphore_signal(barrier, inc=1, device_id={"narrow": other(dx)}, device_id_type=MESH)

    @pl.when(above)
    def _():
        pl.semaphore_signal(barrier, inc=1, device_id={"wide": z + 1}, device_id_type=MESH)

    @pl.when(below)
    def _():
        pl.semaphore_signal(barrier, inc=1, device_id={"wide": z - 1}, device_id_type=MESH)

    sides = jnp.where(below, 1, 0) + jnp.where(above, 1, 0)
    pl.semaphore_wait(barrier, nx - 1 + sides)

    def along(kind, step, source, target):
        return pltpu.make_async_remote_copy(
            src_ref=source,
            dst_ref=target,
            send_sem=halo_send.at[kind],
            recv_sem=halo_recv.at[kind],
            device_id={"wide": z + step},
            device_id_type=MESH,
        )

    def across(kind, dx, source, target):
        return pltpu.make_async_remote_copy(
            src_ref=source,
            dst_ref=target,
            send_sem=cross_send.at[kind, dx],
            recv_sem=cross_recv.at[kind, dx],
            device_id={"narrow": other(dx)},
            device_id_type=MESH,
        )

    first, last = out_ref.at[0, :, mine], out_ref.at[owned + 1, :, mine]
    middle = out_ref.at[pl.ds(1, owned), :, mine]
    up = along(0, 1, state_ref.at[owned - 1], first)
    down = along(1, -1, state_ref.at[0], last)
    right = pltpu.make_async_remote_copy(
        src_ref=packed_ref,
        dst_ref=following_ref,
        send_sem=right_send,
        recv_sem=right_recv,
        device_id={"wide": z - 1},
        device_id_type=MESH,
    )
    own = [across(0, dx, state_ref, middle) for dx in range(1, nx)]
    firsts = [across(1, dx, first, first) for dx in range(1, nx)]
    lasts = [across(2, dx, last, last) for dx in range(1, nx)]
    keep = pltpu.make_async_copy(state_ref, middle, local_sem)

    @pl.when(below)
    def _():
        down.start()

    @pl.when(above)
    def _():
        up.start()

    for one in own:
        one.start()
    keep.start()

    @pl.when(below)
    def _():
        down.wait_send()
        right.start()
        up.wait_recv()
        for one in firsts:
            one.start()

    @pl.when(above)
    def _():
        down.wait_recv()
        for one in lasts:
            one.start()

    spread(rule, {0: mix_zero, 1: mix_up, -1: mix_down})

    keep.wait()
    for one in own:
        one.wait_send()
        one.wait_recv()

    @pl.when(below)
    def _():
        for one in firsts:
            one.wait_send()
            one.wait_recv()
        right.wait_send()

    @pl.when(above)
    def _():
        up.wait_send()
        for one in lasts:
            one.wait_send()
            one.wait_recv()
        right.wait_recv()


def mixer_shape(e):
    return (GROUP * sum(width(x) for _, _, x in blocks[e]), 2 * GROUP * width(e))


def gathered(state, packed, rule):
    owned, phys, rows, cells = state.shape
    nx = lax.axis_size("narrow")
    hbm = pl.BlockSpec(memory_space=pltpu.HBM)
    vmem = pl.BlockSpec(memory_space=pltpu.VMEM)
    dma = pltpu.SemaphoreType.DMA
    return pl.pallas_call(
        gather_kernel,
        out_shape=[
            jax.ShapeDtypeStruct((owned + 2, phys, rows * nx, cells), state.dtype),
            jax.ShapeDtypeStruct(packed.shape, packed.dtype),
        ]
        + [jax.ShapeDtypeStruct(mixer_shape(e), jnp.bfloat16) for e in channel_slices],
        in_specs=[hbm, hbm, vmem],
        out_specs=[hbm, hbm, vmem, vmem, vmem],
        scratch_shapes=[dma, dma((2,)), dma((2,)), dma((3, nx)), dma((3, nx)), dma, dma],
        compiler_params=pltpu.CompilerParams(
            collective_id=0, has_side_effects=True, vmem_limit_bytes=32 * 1024 * 1024
        ),
        name="gather_state",
    )(state, packed, rule)


def apply_kernel(
    count,
    vectors,
    info,
    source,
    left,
    right_same,
    right_next,
    right_last,
    mix_zero,
    mix_up,
    mix_down,
    out,
    passed,
    kept,
    padded,
    mixed,
    combined,
    right,
):
    step = pl.program_id(0)
    rows, bond = left.shape[2], left.shape[3]
    cols = right_same.shape[2]
    chunk = 32 if rows % 32 == 0 else GROUP
    slots = padded.shape[0]
    slot = step + 1
    base = slots + 1
    row_start, col_start = info[base], info[base + 1]
    chosen = info[base + 2 + step]
    mixers = {0: mix_zero, 1: mix_up, -1: mix_down}

    @pl.when(step == 0)
    def _():
        right[:, cols:, :] = jnp.zeros((channel_count, LANES - cols, bond), right.dtype)
        padded[...] = jnp.zeros(padded.shape, padded.dtype)
        col_ids = lax.broadcasted_iota(jnp.int32, (UNIT, cols), 1) + col_start

        def fill(j, carry):
            def fill_unit(u, carry):
                here = pl.ds(pl.multiple_of(u * UNIT, UNIT), UNIT)
                for s in range(PHYS):
                    live = col_ids < info[j + s]
                    for v in range(vectors):
                        part = source[j, s, here, v * cols : (v + 1) * cols].astype(jnp.float32)
                        part = jnp.where(live, part, 0.0).astype(padded.dtype)
                        padded[j, s, here, v * LANES : v * LANES + cols] = part
                return carry

            return lax.fori_loop(0, info[j] // UNIT, fill_unit, carry)

        lax.fori_loop(0, slots, fill, 0)

    live_rows = jnp.clip(info[slot] - row_start, 0, rows) * jnp.where(chosen > 0, 1, 0)

    @pl.when(live_rows == 0)
    def _():
        out[...] = jnp.zeros(out.shape, out.dtype)
        passed[...] = jnp.zeros(passed.shape, passed.dtype)
        kept[...] = jnp.zeros(kept.shape, kept.dtype)

    @pl.when(live_rows > 0)
    def _():
        own_rows = pl.ds(pl.multiple_of(row_start, GROUP), rows)
        for s in range(PHYS):
            for v in range(vectors):
                kept[0, s, v] = padded[slot, s, own_rows, v * LANES : v * LANES + cols]

        def mix(g, carry):
            here = pl.ds(pl.multiple_of(g * GROUP, GROUP), GROUP)
            for e, (low, high) in channel_slices.items():
                block = left[0, low:high, here, :].reshape((high - low) * GROUP, bond)
                block = jnp.concatenate([block, block], 0)
                total = jnp.dot(mixers[e][...], block, preferred_element_type=jnp.float32)
                at = offsets[(e,) + blocks[e][0]]
                n = mixers[e].shape[0] // GROUP
                mixed[at : at + n, here, :] = total.astype(mixed.dtype).reshape(n, GROUP, bond)
            return carry

        lax.fori_loop(0, live_rows // GROUP, mix, 0)
        chunks = live_rows // chunk

        for t in range(PHYS):
            if t == 0:
                right[:, :cols, :] = right_same[0]
            else:

                @pl.when(step < count - 1)
                def _():
                    right[:, :cols, :] = right_next[0]

                @pl.when(step == count - 1)
                def _():
                    pairs = channel_count // 2
                    right[:, :cols, :LANES] = right_last[:channel_count]
                    tails = right_last[channel_count:]
                    right[:pairs, :cols, LANES:] = tails[:, :, : bond - LANES]
                    right[pairs:, :cols, LANES:] = tails[:, :, bond - LANES :]

            def combine(r, carry):
                here = pl.ds(pl.multiple_of(r * chunk, chunk), chunk)
                for x, (low, high) in channel_slices.items():
                    n, total = high - low, None
                    for (e, tt, s, xx), at in offsets.items():
                        if (tt, xx) != (t, x):
                            continue
                        rows_of = mixed[at : at + n, here, :].reshape(n * chunk, bond)
                        term = jnp.dot(
                            rows_of, padded[slot - e, s], preferred_element_type=jnp.float32
                        )
                        total = term if total is None else total + term
                    total = total.astype(combined.dtype)
                    for i in range(n):
                        for v in range(vectors):
                            combined[v, here, (low + i) * LANES : (low + i + 1) * LANES] = total[
                                i * chunk : (i + 1) * chunk, v * LANES : (v + 1) * LANES
                            ]
                return carry

            lax.fori_loop(0, chunks, combine, 0)
            for n in range(1, rows // chunk + 1):

                @pl.when(chunks == n)
                def _(n=n):
                    m = n * chunk
                    total = jnp.dot(
                        combined[:, :m, :].reshape(vectors * m, channel_count * LANES),
                        right[...].reshape(channel_count * LANES, bond),
                        preferred_element_type=jnp.float32,
                    )
                    ids = lax.broadcasted_iota(jnp.int32, (m, cols), 1)
                    low_half = ids < info[slot + t]
                    high_half = ids + cols < info[slot + t]
                    for v in range(vectors):
                        piece = total[v * m : (v + 1) * m]
                        low_piece = jnp.where(low_half, piece[:, :cols], 0.0)
                        high_piece = jnp.where(high_half, piece[:, cols:], 0.0)
                        own = jnp.where(col_start == 0, low_piece, high_piece)
                        sent = jnp.where(col_start == 0, high_piece, low_piece)
                        out[0, t, v, :m, :] = own
                        passed[0, t, v, :m, :] = sent.astype(passed.dtype)
                        if m < rows:
                            rest = (rows - m, cols)
                            out[0, t, v, m:, :] = jnp.zeros(rest, out.dtype)
                            passed[0, t, v, m:, :] = jnp.zeros(rest, passed.dtype)


def applied_parts(info, source, left_env, right_env, right_last, mixers, vectors):
    slots, phys, bond, cells = source.shape
    count = left_env.shape[0]
    rows, cols = left_env.shape[2], right_env.shape[2]

    def whole(array):
        return pl.BlockSpec(array.shape, lambda q, info: (0,) * array.ndim)

    def result(q, info):
        return (q, 0, 0, 0, 0)

    block = (1, phys, vectors, rows, cols)
    full = (count, phys, vectors, rows, cols)
    grid_spec = pltpu.PrefetchScalarGridSpec(
        num_scalar_prefetch=1,
        grid=(count,),
        in_specs=[
            whole(source),
            pl.BlockSpec((1, channel_count, rows, bond), lambda q, info: (q, 0, 0, 0)),
            pl.BlockSpec((1, channel_count, cols, bond), lambda q, info: (q, 0, 0, 0)),
            pl.BlockSpec(
                (1, channel_count, cols, bond),
                lambda q, info: (jnp.minimum(q + 1, count - 1), 0, 0, 0),
            ),
            whole(right_last),
        ]
        + [whole(m) for m in mixers],
        out_specs=[pl.BlockSpec(block, result) for _ in range(3)],
        scratch_shapes=[
            pltpu.VMEM((slots, phys, bond, vectors * LANES), jnp.bfloat16),
            pltpu.VMEM((block_total, rows, bond), jnp.bfloat16),
            pltpu.VMEM((vectors, rows, channel_count * LANES), jnp.bfloat16),
            pltpu.VMEM((channel_count, LANES, bond), jnp.bfloat16),
        ],
    )
    return pl.pallas_call(
        functools.partial(apply_kernel, count, vectors),
        grid_spec=grid_spec,
        out_shape=[
            jax.ShapeDtypeStruct(full, jnp.float32),
            jax.ShapeDtypeStruct(full, jnp.bfloat16),
            jax.ShapeDtypeStruct(full, jnp.bfloat16),
        ],
        compiler_params=pltpu.CompilerParams(
            vmem_limit_bytes=56 * 1024 * 1024, dimension_semantics=("arbitrary",)
        ),
        cost_estimate=pl.CostEstimate(
            flops=5 * 10**9 * count, bytes_accessed=12 * 10**6, transcendentals=0
        ),
        name="apply_sectors",
    )(info, source, left_env, right_env, right_env, right_last, *mixers)


def ratio(top, bottom):
    return jnp.where(bottom > 0, top / jnp.where(bottom > 0, bottom, 1.0), 0.0)


def merged(slots):
    weights = [s[:, 0:1] for s in slots]
    correlations = [s[:, 1:2] for s in slots]
    squares = [s[:, 2:3] for s in slots]
    weight, correlation, squared = sum(weights), sum(correlations), sum(squares)
    center = ratio(correlation, weight)
    for w, c in zip(weights, correlations):
        shift = ratio(c, w) - center
        squared = squared + shift * shift * w
    return weight, correlation, squared


def as_tile(columns):
    lane = lax.broadcasted_iota(jnp.int32, (8, LANES), 1)
    tile = jnp.zeros((8, LANES), jnp.float32)
    for i, column in enumerate(columns):
        tile = jnp.where(lane == i, column, tile)
    return tile


def finish_kernel(
    vectors,
    own_ref,
    passed,
    kept_ref,
    out,
    scalars,
    value_of,
    kept,
    arrived,
    totals,
    near,
    far,
    own_sem,
    kept_sem,
    send_sem,
    recv_sem,
    near_send,
    near_recv,
    far_send,
    far_recv,
):
    nz, nx, nc = lax.axis_size("wide"), lax.axis_size("narrow"), lax.axis_size("rep")
    z, x, c = lax.axis_index("wide"), lax.axis_index("narrow"), lax.axis_index("rep")
    total = nx * nc
    place = x * nc + c
    blocks_here = arrived.shape[0]
    pieces = send_sem.shape[0]
    per_piece = blocks_here // pieces
    loads = []
    for k in range(pieces):
        here = pl.ds(k * per_piece, per_piece)
        loads.append(
            (
                pltpu.make_async_copy(own_ref.at[here], value_of.at[here], own_sem.at[k]),
                pltpu.make_async_copy(kept_ref.at[here], kept.at[here], kept_sem.at[k]),
            )
        )
        for one in loads[-1]:
            one.start()

    def near_id(d):
        target = lax.rem(place + d, total)
        return {"narrow": target // nc, "rep": lax.rem(target, nc)}

    def far_id(d):
        return {"wide": lax.rem(z + d, nz)}

    barrier = pltpu.get_barrier_semaphore()
    for d in range(1, total):
        pl.semaphore_signal(barrier, inc=1, device_id=near_id(d), device_id_type=MESH)
    for d in range(1, nz):
        pl.semaphore_signal(barrier, inc=1, device_id=far_id(d), device_id_type=MESH)
    pl.semaphore_wait(barrier, total + nz - 2)

    exchanges = []
    for k in range(pieces):
        here = pl.ds(k * per_piece, per_piece)
        exchanges.append(
            pltpu.make_async_remote_copy(
                src_ref=passed.at[here],
                dst_ref=arrived.at[here],
                send_sem=send_sem.at[k],
                recv_sem=recv_sem.at[k],
                device_id={"rep": 1 - c},
                device_id_type=MESH,
            )
        )
        exchanges[-1].start()

    shape = arrived.shape[1:]
    totals[...] = jnp.zeros(totals.shape, jnp.float32)
    for k in range(pieces):
        for one in loads[k]:
            one.wait()
        exchanges[k].wait_recv()

        def first_pass(v, carry):
            weight, correlation = totals[0, v], totals[1, v]
            for i in range(per_piece // vectors):
                at = k * per_piece + i * vectors + v
                value = value_of[at] + arrived[at].astype(jnp.float32)
                value_of[at] = value
                state = kept[at].astype(jnp.float32)
                weight += state * state
                correlation += state * value
            totals[0, v] = weight
            totals[1, v] = correlation
            return carry

        lax.fori_loop(0, vectors, first_pass, 0)

    lines = lax.broadcasted_iota(jnp.int32, (8, 1), 0)
    stats = [jnp.zeros((8, 1), jnp.float32) for _ in range(3)]
    for v in range(vectors):
        zero = jnp.zeros(shape, jnp.float32)
        weight = jnp.sum(totals[0, v], keepdims=True)
        correlation = jnp.sum(totals[1, v], keepdims=True)
        center = ratio(correlation, weight)

        def second_pass(i, carry):
            at = i * vectors + v
            rest = value_of[at] - center * kept[at].astype(jnp.float32)
            return carry + rest * rest

        squared = lax.fori_loop(0, blocks_here // vectors, second_pass, zero)
        squared = jnp.sum(squared, keepdims=True)
        for i, value in enumerate((weight, correlation, squared)):
            stats[i] = jnp.where(lines == v, value, stats[i])

    near[place] = as_tile(stats)
    copies = [
        pltpu.make_async_remote_copy(
            src_ref=near.at[place],
            dst_ref=near.at[place],
            send_sem=near_send.at[d],
            recv_sem=near_recv.at[d],
            device_id=near_id(d),
            device_id_type=MESH,
        )
        for d in range(1, total)
    ]
    for one in copies:
        one.start()
    for one in copies:
        one.wait_recv()
    far[z] = as_tile(merged([near[i] for i in range(total)]))
    far_copies = [
        pltpu.make_async_remote_copy(
            src_ref=far.at[z],
            dst_ref=far.at[z],
            send_sem=far_send.at[d],
            recv_sem=far_recv.at[d],
            device_id=far_id(d),
            device_id_type=MESH,
        )
        for d in range(1, nz)
    ]
    for one in far_copies:
        one.start()
    for one in far_copies:
        one.wait_recv()
    weight, correlation, squared = merged([far[i] for i in range(nz)])
    alpha = correlation / weight
    beta = jnp.sqrt((squared + small_term) / weight)
    scalars[...] = as_tile((alpha, beta))
    for v in range(vectors):
        own_alpha, own_beta = alpha[v : v + 1], beta[v : v + 1]

        def last_pass(i, carry):
            at = i * vectors + v
            rest = value_of[at] - own_alpha * kept[at].astype(jnp.float32)
            out[at] = (rest / own_beta).astype(out.dtype)
            return carry

        lax.fori_loop(0, blocks_here // vectors, last_pass, 0)
    for one in exchanges + copies + far_copies:
        one.wait_send()


def finished(own, passed, kept, vectors):
    blocks_here, rows, cols = own.shape
    near_count = lax.axis_size("narrow") * lax.axis_size("rep")
    far_count = lax.axis_size("wide")
    pieces = blocks_here // (PHYS * vectors)
    dma = pltpu.SemaphoreType.DMA
    return pl.pallas_call(
        functools.partial(finish_kernel, vectors),
        out_shape=[
            jax.ShapeDtypeStruct((blocks_here, rows, cols), jnp.bfloat16),
            jax.ShapeDtypeStruct((8, LANES), jnp.float32),
        ],
        in_specs=[pl.BlockSpec(memory_space=pltpu.HBM)] * 3,
        out_specs=[pl.BlockSpec(memory_space=pltpu.VMEM)] * 2,
        scratch_shapes=[
            pltpu.VMEM((blocks_here, rows, cols), jnp.float32),
            pltpu.VMEM((blocks_here, rows, cols), jnp.bfloat16),
            pltpu.VMEM((blocks_here, rows, cols), jnp.bfloat16),
            pltpu.VMEM((2, vectors, rows, cols), jnp.float32),
            pltpu.VMEM((near_count, 8, LANES), jnp.float32),
            pltpu.VMEM((far_count, 8, LANES), jnp.float32),
            dma((pieces,)),
            dma((pieces,)),
            dma((pieces,)),
            dma((pieces,)),
            dma((near_count,)),
            dma((near_count,)),
            dma((far_count,)),
            dma((far_count,)),
        ],
        compiler_params=pltpu.CompilerParams(
            collective_id=1, has_side_effects=True, vmem_limit_bytes=48 * 1024 * 1024
        ),
        name="finish_step",
    )(own, passed, kept)


def body(state, left_env, right_env, mpo_tensor, sector_units, chosen):
    owned, phys, rows, vectors, cols = state.shape
    first_sector = lax.axis_index("wide") * owned
    row_start = lax.axis_index("narrow") * rows
    col_start = lax.axis_index("rep") * cols
    none = jnp.zeros((1,), jnp.int32)
    sizes = jnp.concatenate([none, sector_units * UNIT, none, none])
    info = jnp.concatenate(
        [
            lax.dynamic_slice_in_dim(sizes, first_sector, owned + 3),
            row_start[None],
            col_start[None],
            lax.dynamic_slice_in_dim(chosen, first_sector, owned),
        ]
    ).astype(jnp.int32)
    rule = jnp.transpose(mpo_tensor, (2, 3, 1, 0))
    source, following, *mixers = gathered(
        state.reshape(owned, phys, rows, vectors * cols), packed_lanes(right_env[0]), rule
    )
    parts = applied_parts(info, source, left_env, right_env, following, mixers, vectors)
    out, scalars = finished(
        *(part.reshape(owned * phys * vectors, rows, cols) for part in parts), vectors
    )
    next_state = out.reshape(owned, phys, vectors, rows, cols).transpose(0, 1, 3, 2, 4)
    return (next_state, scalars[:vectors, 0], scalars[:vectors, 1])


def solution(mesh):
    placed = (
        P(("groups", "wide"), None, "narrow", None, "rep"),
        P(("groups", "wide"), None, "narrow", None),
        P(("groups", "wide"), None, "rep", None),
        P(),
        P("groups"),
        P("groups"),
    )
    return jax.shard_map(
        body,
        mesh=mesh,
        in_specs=placed,
        out_specs=(P(("groups", "wide"), None, "narrow", None, "rep"), P("groups"), P("groups")),
        check_vma=False,
    )
```

```python
import functools
import jax
import jax.numpy as jnp
from jax import lax
from jax.experimental import pallas as pl
from jax.experimental.pallas import tpu as pltpu
from jax.sharding import PartitionSpec as P

UNIT = 32
PHYS = 2
LANES = 128
GROUP = 16
MESH = pl.DeviceIdType.MESH

small_term = 1e-06
channel_slices = {0: (0, 10), 1: (10, 17), -1: (17, 24)}
channel_count = 24
blocks = {
    0: ((0, 0, 0), (1, 1, 0), (1, 0, 1), (0, 1, -1)),
    1: ((0, 0, 1), (1, 1, 1), (0, 1, 0)),
    -1: ((0, 0, -1), (1, 1, -1), (1, 0, 0)),
}


def width(charge):
    low, high = channel_slices[charge]
    return high - low


def block_table():
    table, at = {}, 0
    for e, entries in blocks.items():
        for t, s, x in entries:
            table[(e, t, s, x)] = at
            at += width(x)
    return table, at


offsets, block_total = block_table()


def packed_lanes(block):
    half = block.shape[0] // 2
    rest = block[:, :, LANES:]
    return jnp.concatenate(
        [block[:, :, :LANES], jnp.concatenate([rest[:half], rest[half:]], 2)], 0
    )


def spread(rule, mixers):
    for e, (low, high) in channel_slices.items():
        n, depth = high - low, 2 * (high - low) * GROUP
        at = 0
        for t, s, x in blocks[e]:
            x_low, x_high = channel_slices[x]
            m = x_high - x_low
            exact = rule[t, s, x_low:x_high, low:high]
            coarse = exact.astype(jnp.bfloat16)
            rest = (exact - coarse.astype(jnp.float32)).astype(jnp.bfloat16)
            row = lax.broadcasted_iota(jnp.int32, (m * GROUP, m), 0) // GROUP
            up = jnp.where(row == lax.broadcasted_iota(jnp.int32, (m * GROUP, m), 1), 1.0, 0.0)
            up = up.astype(jnp.bfloat16)
            col = lax.broadcasted_iota(jnp.int32, (n, depth), 1) // GROUP
            line = lax.broadcasted_iota(jnp.int32, (n, depth), 0)
            total = None
            for part, start in ((coarse, 0), (rest, n)):
                side = jnp.where(col == line + start, 1.0, 0.0).astype(jnp.bfloat16)
                tall = jnp.dot(up, part, preferred_element_type=jnp.float32).astype(jnp.bfloat16)
                term = jnp.dot(tall, side, preferred_element_type=jnp.float32)
                total = term if total is None else total + term
            shape = (m * GROUP, depth)
            same = lax.broadcasted_iota(jnp.int32, shape, 0) % GROUP == (
                lax.broadcasted_iota(jnp.int32, shape, 1) % GROUP
            )
            mixers[e][at : at + m * GROUP, :] = jnp.where(same, total, 0.0).astype(jnp.bfloat16)
            at += m * GROUP


def gather_kernel(
    state_ref,
    packed_ref,
    rule,
    out_ref,
    following_ref,
    mix_zero,
    mix_up,
    mix_down,
    local_sem,
    halo_send,
    halo_recv,
    cross_send,
    cross_recv,
    right_send,
    right_recv,
):
    nz, nx = lax.axis_size("wide"), lax.axis_size("narrow")
    z, x = lax.axis_index("wide"), lax.axis_index("narrow")
    owned, _, rows, _ = state_ref.shape
    mine = pl.ds(pl.multiple_of(x * rows, GROUP), rows)
    below, above = z > 0, z < nz - 1

    def other(dx):
        return lax.rem(x + dx, nx)

    barrier = pltpu.get_barrier_semaphore()
    for dx in range(1, nx):
        pl.semaphore_signal(barrier, inc=1, device_id={"narrow": other(dx)}, device_id_type=MESH)

    @pl.when(above)
    def _():
        pl.semaphore_signal(barrier, inc=1, device_id={"wide": z + 1}, device_id_type=MESH)

    @pl.when(below)
    def _():
        pl.semaphore_signal(barrier, inc=1, device_id={"wide": z - 1}, device_id_type=MESH)

    sides = jnp.where(below, 1, 0) + jnp.where(above, 1, 0)
    pl.semaphore_wait(barrier, nx - 1 + sides)

    def along(kind, step, source, target):
        return pltpu.make_async_remote_copy(
            src_ref=source,
            dst_ref=target,
            send_sem=halo_send.at[kind],
            recv_sem=halo_recv.at[kind],
            device_id={"wide": z + step},
            device_id_type=MESH,
        )

    def across(kind, dx, source, target):
        return pltpu.make_async_remote_copy(
            src_ref=source,
            dst_ref=target,
            send_sem=cross_send.at[kind, dx],
            recv_sem=cross_recv.at[kind, dx],
            device_id={"narrow": other(dx)},
            device_id_type=MESH,
        )

    first, last = out_ref.at[0, :, mine], out_ref.at[owned + 1, :, mine]
    middle = out_ref.at[pl.ds(1, owned), :, mine]
    up = along(0, 1, state_ref.at[owned - 1], first)
    down = along(1, -1, state_ref.at[0], last)
    right = pltpu.make_async_remote_copy(
        src_ref=packed_ref,
        dst_ref=following_ref,
        send_sem=right_send,
        recv_sem=right_recv,
        device_id={"wide": z - 1},
        device_id_type=MESH,
    )
    own = [across(0, dx, state_ref, middle) for dx in range(1, nx)]
    firsts = [across(1, dx, first, first) for dx in range(1, nx)]
    lasts = [across(2, dx, last, last) for dx in range(1, nx)]
    keep = pltpu.make_async_copy(state_ref, middle, local_sem)

    @pl.when(below)
    def _():
        down.start()

    @pl.when(above)
    def _():
        up.start()

    for one in own:
        one.start()
    keep.start()

    @pl.when(below)
    def _():
        down.wait_send()
        right.start()
        up.wait_recv()
        for one in firsts:
            one.start()

    @pl.when(above)
    def _():
        down.wait_recv()
        for one in lasts:
            one.start()

    spread(rule, {0: mix_zero, 1: mix_up, -1: mix_down})

    keep.wait()
    for one in own:
        one.wait_send()
        one.wait_recv()

    @pl.when(below)
    def _():
        for one in firsts:
            one.wait_send()
            one.wait_recv()
        right.wait_send()

    @pl.when(above)
    def _():
        up.wait_send()
        for one in lasts:
            one.wait_send()
            one.wait_recv()
        right.wait_recv()


def mixer_shape(e):
    return (GROUP * sum(width(x) for _, _, x in blocks[e]), 2 * GROUP * width(e))


def gathered(state, packed, rule):
    owned, phys, rows, cells = state.shape
    nx = lax.axis_size("narrow")
    hbm = pl.BlockSpec(memory_space=pltpu.HBM)
    vmem = pl.BlockSpec(memory_space=pltpu.VMEM)
    dma = pltpu.SemaphoreType.DMA
    return pl.pallas_call(
        gather_kernel,
        out_shape=[
            jax.ShapeDtypeStruct((owned + 2, phys, rows * nx, cells), state.dtype),
            jax.ShapeDtypeStruct(packed.shape, packed.dtype),
        ]
        + [jax.ShapeDtypeStruct(mixer_shape(e), jnp.bfloat16) for e in channel_slices],
        in_specs=[hbm, hbm, vmem],
        out_specs=[hbm, hbm, vmem, vmem, vmem],
        scratch_shapes=[dma, dma((2,)), dma((2,)), dma((3, nx)), dma((3, nx)), dma, dma],
        compiler_params=pltpu.CompilerParams(
            collective_id=0, has_side_effects=True, vmem_limit_bytes=12 * 1024 * 1024
        ),
        name="gather_state",
    )(state, packed, rule)


def apply_kernel(
    count,
    vectors,
    info,
    source,
    left,
    right_same,
    right_next,
    right_last,
    mix_zero,
    mix_up,
    mix_down,
    out,
    passed,
    kept,
    padded,
    mixed,
    combined,
    right,
):
    step = pl.program_id(0)
    rows, bond = left.shape[2], left.shape[3]
    cols = right_same.shape[2]
    chunk = 32 if rows % 32 == 0 else GROUP
    slots = padded.shape[0]
    slot = step + 1
    base = slots + 1
    row_start, col_start = info[base], info[base + 1]
    chosen = info[base + 2 + step]
    mixers = {0: mix_zero, 1: mix_up, -1: mix_down}

    @pl.when(step == 0)
    def _():
        right[:, cols:, :] = jnp.zeros((channel_count, LANES - cols, bond), right.dtype)
        padded[...] = jnp.zeros(padded.shape, padded.dtype)
        col_ids = lax.broadcasted_iota(jnp.int32, (UNIT, cols), 1) + col_start

        def fill(j, carry):
            def fill_unit(u, carry):
                here = pl.ds(pl.multiple_of(u * UNIT, UNIT), UNIT)
                for s in range(PHYS):
                    live = col_ids < info[j + s]
                    for v in range(vectors):
                        part = source[j, s, here, v * cols : (v + 1) * cols].astype(jnp.float32)
                        part = jnp.where(live, part, 0.0).astype(padded.dtype)
                        padded[j, s, here, v * LANES : v * LANES + cols] = part
                return carry

            return lax.fori_loop(0, info[j] // UNIT, fill_unit, carry)

        lax.fori_loop(0, slots, fill, 0)

    live_rows = jnp.clip(info[slot] - row_start, 0, rows) * jnp.where(chosen > 0, 1, 0)

    @pl.when(live_rows == 0)
    def _():
        out[...] = jnp.zeros(out.shape, out.dtype)
        passed[...] = jnp.zeros(passed.shape, passed.dtype)
        kept[...] = jnp.zeros(kept.shape, kept.dtype)

    @pl.when(live_rows > 0)
    def _():
        own_rows = pl.ds(pl.multiple_of(row_start, GROUP), rows)
        for s in range(PHYS):
            for v in range(vectors):
                kept[0, s, v] = padded[slot, s, own_rows, v * LANES : v * LANES + cols]

        def mix(g, carry):
            here = pl.ds(pl.multiple_of(g * GROUP, GROUP), GROUP)
            for e, (low, high) in channel_slices.items():
                block = left[0, low:high, here, :].reshape((high - low) * GROUP, bond)
                block = jnp.concatenate([block, block], 0)
                total = jnp.dot(mixers[e][...], block, preferred_element_type=jnp.float32)
                at = offsets[(e,) + blocks[e][0]]
                n = mixers[e].shape[0] // GROUP
                mixed[at : at + n, here, :] = total.astype(mixed.dtype).reshape(n, GROUP, bond)
            return carry

        lax.fori_loop(0, live_rows // GROUP, mix, 0)
        chunks = live_rows // chunk

        for t in range(PHYS):
            if t == 0:
                right[:, :cols, :] = right_same[0]
            else:

                @pl.when(step < count - 1)
                def _():
                    right[:, :cols, :] = right_next[0]

                @pl.when(step == count - 1)
                def _():
                    pairs = channel_count // 2
                    right[:, :cols, :LANES] = right_last[:channel_count]
                    tails = right_last[channel_count:]
                    right[:pairs, :cols, LANES:] = tails[:, :, : bond - LANES]
                    right[pairs:, :cols, LANES:] = tails[:, :, bond - LANES :]

            def combine(r, carry):
                here = pl.ds(pl.multiple_of(r * chunk, chunk), chunk)
                for x, (low, high) in channel_slices.items():
                    n, total = high - low, None
                    for (e, tt, s, xx), at in offsets.items():
                        if (tt, xx) != (t, x):
                            continue
                        rows_of = mixed[at : at + n, here, :].reshape(n * chunk, bond)
                        term = jnp.dot(
                            rows_of, padded[slot - e, s], preferred_element_type=jnp.float32
                        )
                        total = term if total is None else total + term
                    total = total.astype(combined.dtype)
                    for i in range(n):
                        for v in range(vectors):
                            combined[v, here, (low + i) * LANES : (low + i + 1) * LANES] = total[
                                i * chunk : (i + 1) * chunk, v * LANES : (v + 1) * LANES
                            ]
                return carry

            lax.fori_loop(0, chunks, combine, 0)
            for n in range(1, rows // chunk + 1):

                @pl.when(chunks == n)
                def _(n=n):
                    m = n * chunk
                    total = jnp.dot(
                        combined[:, :m, :].reshape(vectors * m, channel_count * LANES),
                        right[...].reshape(channel_count * LANES, bond),
                        preferred_element_type=jnp.float32,
                    )
                    ids = lax.broadcasted_iota(jnp.int32, (m, cols), 1)
                    low_half = ids < info[slot + t]
                    high_half = ids + cols < info[slot + t]
                    for v in range(vectors):
                        piece = total[v * m : (v + 1) * m]
                        low_piece = jnp.where(low_half, piece[:, :cols], 0.0)
                        high_piece = jnp.where(high_half, piece[:, cols:], 0.0)
                        own = jnp.where(col_start == 0, low_piece, high_piece)
                        sent = jnp.where(col_start == 0, high_piece, low_piece)
                        out[0, t, v, :m, :] = own
                        passed[0, t, v, :m, :] = sent.astype(passed.dtype)
                        if m < rows:
                            rest = (rows - m, cols)
                            out[0, t, v, m:, :] = jnp.zeros(rest, out.dtype)
                            passed[0, t, v, m:, :] = jnp.zeros(rest, passed.dtype)


def applied_parts(info, source, left_env, right_env, right_last, mixers, vectors):
    slots, phys, bond, cells = source.shape
    count = left_env.shape[0]
    rows, cols = left_env.shape[2], right_env.shape[2]

    def whole(array):
        return pl.BlockSpec(array.shape, lambda q, info: (0,) * array.ndim)

    def result(q, info):
        return (q, 0, 0, 0, 0)

    block = (1, phys, vectors, rows, cols)
    full = (count, phys, vectors, rows, cols)
    grid_spec = pltpu.PrefetchScalarGridSpec(
        num_scalar_prefetch=1,
        grid=(count,),
        in_specs=[
            whole(source),
            pl.BlockSpec((1, channel_count, rows, bond), lambda q, info: (q, 0, 0, 0)),
            pl.BlockSpec((1, channel_count, cols, bond), lambda q, info: (q, 0, 0, 0)),
            pl.BlockSpec(
                (1, channel_count, cols, bond),
                lambda q, info: (jnp.minimum(q + 1, count - 1), 0, 0, 0),
            ),
            whole(right_last),
        ]
        + [whole(m) for m in mixers],
        out_specs=[pl.BlockSpec(block, result) for _ in range(3)],
        scratch_shapes=[
            pltpu.VMEM((slots, phys, bond, vectors * LANES), jnp.bfloat16),
            pltpu.VMEM((block_total, rows, bond), jnp.bfloat16),
            pltpu.VMEM((vectors, rows, channel_count * LANES), jnp.bfloat16),
            pltpu.VMEM((channel_count, LANES, bond), jnp.bfloat16),
        ],
    )
    return pl.pallas_call(
        functools.partial(apply_kernel, count, vectors),
        grid_spec=grid_spec,
        out_shape=[
            jax.ShapeDtypeStruct(full, jnp.float32),
            jax.ShapeDtypeStruct(full, jnp.bfloat16),
            jax.ShapeDtypeStruct(full, jnp.bfloat16),
        ],
        compiler_params=pltpu.CompilerParams(
            vmem_limit_bytes=38 * 1024 * 1024, dimension_semantics=("arbitrary",)
        ),
        cost_estimate=pl.CostEstimate(
            flops=5 * 10**9 * count, bytes_accessed=12 * 10**6, transcendentals=0
        ),
        name="apply_sectors",
    )(info, source, left_env, right_env, right_env, right_last, *mixers)


def ratio(top, bottom):
    return jnp.where(bottom > 0, top / jnp.where(bottom > 0, bottom, 1.0), 0.0)


def merged(slots):
    weights = [s[:, 0:1] for s in slots]
    correlations = [s[:, 1:2] for s in slots]
    squares = [s[:, 2:3] for s in slots]
    weight, correlation, squared = sum(weights), sum(correlations), sum(squares)
    center = ratio(correlation, weight)
    for w, c in zip(weights, correlations):
        shift = ratio(c, w) - center
        squared = squared + shift * shift * w
    return weight, correlation, squared


def as_tile(columns):
    lane = lax.broadcasted_iota(jnp.int32, (8, LANES), 1)
    tile = jnp.zeros((8, LANES), jnp.float32)
    for i, column in enumerate(columns):
        tile = jnp.where(lane == i, column, tile)
    return tile


def finish_kernel(
    vectors,
    own_ref,
    passed,
    kept_ref,
    out,
    scalars,
    value_of,
    kept,
    arrived,
    totals,
    near,
    far,
    own_sem,
    kept_sem,
    send_sem,
    recv_sem,
    near_send,
    near_recv,
    far_send,
    far_recv,
):
    nz, nx, nc = lax.axis_size("wide"), lax.axis_size("narrow"), lax.axis_size("rep")
    z, x, c = lax.axis_index("wide"), lax.axis_index("narrow"), lax.axis_index("rep")
    total = nx * nc
    place = x * nc + c
    blocks_here = arrived.shape[0]
    pieces = send_sem.shape[0]
    per_piece = blocks_here // pieces
    loads = []
    for k in range(pieces):
        here = pl.ds(k * per_piece, per_piece)
        loads.append(
            (
                pltpu.make_async_copy(own_ref.at[here], value_of.at[here], own_sem.at[k]),
                pltpu.make_async_copy(kept_ref.at[here], kept.at[here], kept_sem.at[k]),
            )
        )
        for one in loads[-1]:
            one.start()

    def near_id(d):
        target = lax.rem(place + d, total)
        return {"narrow": target // nc, "rep": lax.rem(target, nc)}

    def far_id(d):
        return {"wide": lax.rem(z + d, nz)}

    barrier = pltpu.get_barrier_semaphore()
    for d in range(1, total):
        pl.semaphore_signal(barrier, inc=1, device_id=near_id(d), device_id_type=MESH)
    for d in range(1, nz):
        pl.semaphore_signal(barrier, inc=1, device_id=far_id(d), device_id_type=MESH)
    pl.semaphore_wait(barrier, total + nz - 2)

    exchanges = []
    for k in range(pieces):
        here = pl.ds(k * per_piece, per_piece)
        exchanges.append(
            pltpu.make_async_remote_copy(
                src_ref=passed.at[here],
                dst_ref=arrived.at[here],
                send_sem=send_sem.at[k],
                recv_sem=recv_sem.at[k],
                device_id={"rep": 1 - c},
                device_id_type=MESH,
            )
        )
        exchanges[-1].start()

    shape = arrived.shape[1:]
    totals[...] = jnp.zeros(totals.shape, jnp.float32)
    for k in range(pieces):
        for one in loads[k]:
            one.wait()
        exchanges[k].wait_recv()

        def first_pass(v, carry):
            weight, correlation = totals[0, v], totals[1, v]
            for i in range(per_piece // vectors):
                at = k * per_piece + i * vectors + v
                value = value_of[at] + arrived[at].astype(jnp.float32)
                value_of[at] = value
                state = kept[at].astype(jnp.float32)
                weight += state * state
                correlation += state * value
            totals[0, v] = weight
            totals[1, v] = correlation
            return carry

        lax.fori_loop(0, vectors, first_pass, 0)

    lines = lax.broadcasted_iota(jnp.int32, (8, 1), 0)
    stats = [jnp.zeros((8, 1), jnp.float32) for _ in range(3)]
    for v in range(vectors):
        zero = jnp.zeros(shape, jnp.float32)
        weight = jnp.sum(totals[0, v], keepdims=True)
        correlation = jnp.sum(totals[1, v], keepdims=True)
        center = ratio(correlation, weight)

        def second_pass(i, carry):
            at = i * vectors + v
            rest = value_of[at] - center * kept[at].astype(jnp.float32)
            return carry + rest * rest

        squared = lax.fori_loop(0, blocks_here // vectors, second_pass, zero)
        squared = jnp.sum(squared, keepdims=True)
        for i, value in enumerate((weight, correlation, squared)):
            stats[i] = jnp.where(lines == v, value, stats[i])

    near[place] = as_tile(stats)
    copies = [
        pltpu.make_async_remote_copy(
            src_ref=near.at[place],
            dst_ref=near.at[place],
            send_sem=near_send.at[d],
            recv_sem=near_recv.at[d],
            device_id=near_id(d),
            device_id_type=MESH,
        )
        for d in range(1, total)
    ]
    for one in copies:
        one.start()
    for one in copies:
        one.wait_recv()
    far[z] = as_tile(merged([near[i] for i in range(total)]))
    far_copies = [
        pltpu.make_async_remote_copy(
            src_ref=far.at[z],
            dst_ref=far.at[z],
            send_sem=far_send.at[d],
            recv_sem=far_recv.at[d],
            device_id=far_id(d),
            device_id_type=MESH,
        )
        for d in range(1, nz)
    ]
    for one in far_copies:
        one.start()
    for one in far_copies:
        one.wait_recv()
    weight, correlation, squared = merged([far[i] for i in range(nz)])
    alpha = correlation / weight
    beta = jnp.sqrt((squared + small_term) / weight)
    scalars[...] = as_tile((alpha, beta))
    for v in range(vectors):
        own_alpha, own_beta = alpha[v : v + 1], beta[v : v + 1]

        def last_pass(i, carry):
            at = i * vectors + v
            rest = value_of[at] - own_alpha * kept[at].astype(jnp.float32)
            out[at] = (rest / own_beta).astype(out.dtype)
            return carry

        lax.fori_loop(0, blocks_here // vectors, last_pass, 0)
    for one in exchanges + copies + far_copies:
        one.wait_send()


def finished(own, passed, kept, vectors):
    blocks_here, rows, cols = own.shape
    near_count = lax.axis_size("narrow") * lax.axis_size("rep")
    far_count = lax.axis_size("wide")
    pieces = blocks_here // (PHYS * vectors)
    dma = pltpu.SemaphoreType.DMA
    return pl.pallas_call(
        functools.partial(finish_kernel, vectors),
        out_shape=[
            jax.ShapeDtypeStruct((blocks_here, rows, cols), jnp.bfloat16),
            jax.ShapeDtypeStruct((8, LANES), jnp.float32),
        ],
        in_specs=[pl.BlockSpec(memory_space=pltpu.HBM)] * 3,
        out_specs=[pl.BlockSpec(memory_space=pltpu.VMEM)] * 2,
        scratch_shapes=[
            pltpu.VMEM((blocks_here, rows, cols), jnp.float32),
            pltpu.VMEM((blocks_here, rows, cols), jnp.bfloat16),
            pltpu.VMEM((blocks_here, rows, cols), jnp.bfloat16),
            pltpu.VMEM((2, vectors, rows, cols), jnp.float32),
            pltpu.VMEM((near_count, 8, LANES), jnp.float32),
            pltpu.VMEM((far_count, 8, LANES), jnp.float32),
            dma((pieces,)),
            dma((pieces,)),
            dma((pieces,)),
            dma((pieces,)),
            dma((near_count,)),
            dma((near_count,)),
            dma((far_count,)),
            dma((far_count,)),
        ],
        compiler_params=pltpu.CompilerParams(
            collective_id=1, has_side_effects=True, vmem_limit_bytes=14 * 1024 * 1024
        ),
        name="finish_step",
    )(own, passed, kept)


def body(state, left_env, right_env, mpo_tensor, sector_units, chosen):
    owned, phys, rows, vectors, cols = state.shape
    first_sector = lax.axis_index("wide") * owned
    row_start = lax.axis_index("narrow") * rows
    col_start = lax.axis_index("rep") * cols
    none = jnp.zeros((1,), jnp.int32)
    sizes = jnp.concatenate([none, sector_units * UNIT, none, none])
    info = jnp.concatenate(
        [
            lax.dynamic_slice_in_dim(sizes, first_sector, owned + 3),
            row_start[None],
            col_start[None],
            lax.dynamic_slice_in_dim(chosen, first_sector, owned),
        ]
    ).astype(jnp.int32)
    rule = jnp.transpose(mpo_tensor, (2, 3, 1, 0))
    source, following, *mixers = gathered(
        state.reshape(owned, phys, rows, vectors * cols), packed_lanes(right_env[0]), rule
    )
    parts = applied_parts(info, source, left_env, right_env, following, mixers, vectors)
    out, scalars = finished(
        *(part.reshape(owned * phys * vectors, rows, cols) for part in parts), vectors
    )
    next_state = out.reshape(owned, phys, vectors, rows, cols).transpose(0, 1, 3, 2, 4)
    return (next_state, scalars[:vectors, 0], scalars[:vectors, 1])


def solution(mesh):
    placed = (
        P(("groups", "wide"), None, "narrow", None, "rep"),
        P(("groups", "wide"), None, "narrow", None),
        P(("groups", "wide"), None, "rep", None),
        P(),
        P("groups"),
        P("groups"),
    )
    return jax.shard_map(
        body,
        mesh=mesh,
        in_specs=placed,
        out_specs=(P(("groups", "wide"), None, "narrow", None, "rep"), P("groups"), P("groups")),
        check_vma=False,
    )
```

```python
import functools
import jax
import jax.numpy as jnp
from jax import lax
from jax.experimental import pallas as pl
from jax.experimental.pallas import tpu as pltpu
from jax.sharding import PartitionSpec as P

UNIT = 32
PHYS = 2
LANES = 128
GROUP = 16
MESH = pl.DeviceIdType.MESH

small_term = 1e-06
channel_slices = {0: (0, 10), 1: (10, 17), -1: (17, 24)}
channel_count = 24
blocks = {
    0: ((0, 0, 0), (1, 1, 0), (1, 0, 1), (0, 1, -1)),
    1: ((0, 0, 1), (1, 1, 1), (0, 1, 0)),
    -1: ((0, 0, -1), (1, 1, -1), (1, 0, 0)),
}


def width(charge):
    low, high = channel_slices[charge]
    return high - low


def block_table():
    table, at = {}, 0
    for e, entries in blocks.items():
        for t, s, x in entries:
            table[(e, t, s, x)] = at
            at += width(x)
    return table, at


offsets, block_total = block_table()


def packed_lanes(block):
    half = block.shape[0] // 2
    rest = block[:, :, LANES:]
    return jnp.concatenate(
        [block[:, :, :LANES], jnp.concatenate([rest[:half], rest[half:]], 2)], 0
    )


def spread(rule, mixers):
    for e, (low, high) in channel_slices.items():
        n, depth = high - low, 2 * (high - low) * GROUP
        at = 0
        for t, s, x in blocks[e]:
            x_low, x_high = channel_slices[x]
            m = x_high - x_low
            exact = rule[t, s, x_low:x_high, low:high]
            coarse = exact.astype(jnp.bfloat16)
            rest = (exact - coarse.astype(jnp.float32)).astype(jnp.bfloat16)
            row = lax.broadcasted_iota(jnp.int32, (m * GROUP, m), 0) // GROUP
            up = jnp.where(row == lax.broadcasted_iota(jnp.int32, (m * GROUP, m), 1), 1.0, 0.0)
            up = up.astype(jnp.bfloat16)
            col = lax.broadcasted_iota(jnp.int32, (n, depth), 1) // GROUP
            line = lax.broadcasted_iota(jnp.int32, (n, depth), 0)
            total = None
            for part, start in ((coarse, 0), (rest, n)):
                side = jnp.where(col == line + start, 1.0, 0.0).astype(jnp.bfloat16)
                tall = jnp.dot(up, part, preferred_element_type=jnp.float32).astype(jnp.bfloat16)
                term = jnp.dot(tall, side, preferred_element_type=jnp.float32)
                total = term if total is None else total + term
            shape = (m * GROUP, depth)
            same = lax.broadcasted_iota(jnp.int32, shape, 0) % GROUP == (
                lax.broadcasted_iota(jnp.int32, shape, 1) % GROUP
            )
            mixers[e][at : at + m * GROUP, :] = jnp.where(same, total, 0.0).astype(jnp.bfloat16)
            at += m * GROUP


def gather_kernel(
    state_ref,
    packed_ref,
    rule,
    out_ref,
    following_ref,
    mix_zero,
    mix_up,
    mix_down,
    local_sem,
    halo_send,
    halo_recv,
    cross_send,
    cross_recv,
    right_send,
    right_recv,
):
    nz, nx = lax.axis_size("wide"), lax.axis_size("narrow")
    z, x = lax.axis_index("wide"), lax.axis_index("narrow")
    owned, _, rows, _ = state_ref.shape
    mine = pl.ds(pl.multiple_of(x * rows, GROUP), rows)
    below, above = z > 0, z < nz - 1

    def other(dx):
        return lax.rem(x + dx, nx)

    barrier = pltpu.get_barrier_semaphore()
    for dx in range(1, nx):
        pl.semaphore_signal(barrier, inc=1, device_id={"narrow": other(dx)}, device_id_type=MESH)

    @pl.when(above)
    def _():
        pl.semaphore_signal(barrier, inc=1, device_id={"wide": z + 1}, device_id_type=MESH)

    @pl.when(below)
    def _():
        pl.semaphore_signal(barrier, inc=1, device_id={"wide": z - 1}, device_id_type=MESH)

    sides = jnp.where(below, 1, 0) + jnp.where(above, 1, 0)
    pl.semaphore_wait(barrier, nx - 1 + sides)

    def along(kind, step, source, target):
        return pltpu.make_async_remote_copy(
            src_ref=source,
            dst_ref=target,
            send_sem=halo_send.at[kind],
            recv_sem=halo_recv.at[kind],
            device_id={"wide": z + step},
            device_id_type=MESH,
        )

    def across(kind, dx, source, target):
        return pltpu.make_async_remote_copy(
            src_ref=source,
            dst_ref=target,
            send_sem=cross_send.at[kind, dx],
            recv_sem=cross_recv.at[kind, dx],
            device_id={"narrow": other(dx)},
            device_id_type=MESH,
        )

    first, last = out_ref.at[0, :, mine], out_ref.at[owned + 1, :, mine]
    middle = out_ref.at[pl.ds(1, owned), :, mine]
    up = along(0, 1, state_ref.at[owned - 1], first)
    down = along(1, -1, state_ref.at[0], last)
    right = pltpu.make_async_remote_copy(
        src_ref=packed_ref,
        dst_ref=following_ref,
        send_sem=right_send,
        recv_sem=right_recv,
        device_id={"wide": z - 1},
        device_id_type=MESH,
    )
    own = [across(0, dx, state_ref, middle) for dx in range(1, nx)]
    firsts = [across(1, dx, first, first) for dx in range(1, nx)]
    lasts = [across(2, dx, last, last) for dx in range(1, nx)]
    keep = pltpu.make_async_copy(state_ref, middle, local_sem)

    @pl.when(below)
    def _():
        down.start()
        right.start()

    @pl.when(above)
    def _():
        up.start()

    for one in own:
        one.start()
    keep.start()

    @pl.when(below)
    def _():
        up.wait_recv()
        for one in firsts:
            one.start()

    @pl.when(above)
    def _():
        down.wait_recv()
        for one in lasts:
            one.start()

    spread(rule, {0: mix_zero, 1: mix_up, -1: mix_down})

    keep.wait()
    for one in own:
        one.wait_send()
        one.wait_recv()

    @pl.when(below)
    def _():
        for one in firsts:
            one.wait_send()
            one.wait_recv()
        down.wait_send()
        right.wait_send()

    @pl.when(above)
    def _():
        up.wait_send()
        for one in lasts:
            one.wait_send()
            one.wait_recv()
        right.wait_recv()


def mixer_shape(e):
    return (GROUP * sum(width(x) for _, _, x in blocks[e]), 2 * GROUP * width(e))


def gathered(state, packed, rule):
    owned, phys, rows, cells = state.shape
    nx = lax.axis_size("narrow")
    hbm = pl.BlockSpec(memory_space=pltpu.HBM)
    vmem = pl.BlockSpec(memory_space=pltpu.VMEM)
    dma = pltpu.SemaphoreType.DMA
    return pl.pallas_call(
        gather_kernel,
        out_shape=[
            jax.ShapeDtypeStruct((owned + 2, phys, rows * nx, cells), state.dtype),
            jax.ShapeDtypeStruct(packed.shape, packed.dtype),
        ]
        + [jax.ShapeDtypeStruct(mixer_shape(e), jnp.bfloat16) for e in channel_slices],
        in_specs=[hbm, hbm, vmem],
        out_specs=[hbm, hbm, vmem, vmem, vmem],
        scratch_shapes=[dma, dma((2,)), dma((2,)), dma((3, nx)), dma((3, nx)), dma, dma],
        compiler_params=pltpu.CompilerParams(
            collective_id=0, has_side_effects=True, vmem_limit_bytes=12 * 1024 * 1024
        ),
        name="gather_state",
    )(state, packed, rule)


def apply_kernel(
    count,
    vectors,
    info,
    source,
    left,
    right_same,
    right_next,
    right_last,
    mix_zero,
    mix_up,
    mix_down,
    out,
    passed,
    kept,
    padded,
    mixed,
    combined,
    right,
):
    step = pl.program_id(0)
    rows, bond = left.shape[2], left.shape[3]
    cols = right_same.shape[2]
    chunk = 32 if rows % 32 == 0 else GROUP
    slots = padded.shape[0]
    slot = step + 1
    base = slots + 1
    row_start, col_start = info[base], info[base + 1]
    chosen = info[base + 2 + step]
    mixers = {0: mix_zero, 1: mix_up, -1: mix_down}

    @pl.when(step == 0)
    def _():
        right[:, cols:, :] = jnp.zeros((channel_count, LANES - cols, bond), right.dtype)
        padded[...] = jnp.zeros(padded.shape, padded.dtype)
        col_ids = lax.broadcasted_iota(jnp.int32, (UNIT, cols), 1) + col_start

        def fill(j, carry):
            def fill_unit(u, carry):
                here = pl.ds(pl.multiple_of(u * UNIT, UNIT), UNIT)
                for s in range(PHYS):
                    live = col_ids < info[j + s]
                    for v in range(vectors):
                        part = source[j, s, here, v * cols : (v + 1) * cols].astype(jnp.float32)
                        part = jnp.where(live, part, 0.0).astype(padded.dtype)
                        padded[j, s, here, v * LANES : v * LANES + cols] = part
                return carry

            return lax.fori_loop(0, info[j] // UNIT, fill_unit, carry)

        lax.fori_loop(0, slots, fill, 0)

    live_rows = jnp.clip(info[slot] - row_start, 0, rows) * jnp.where(chosen > 0, 1, 0)

    @pl.when(live_rows == 0)
    def _():
        out[...] = jnp.zeros(out.shape, out.dtype)
        passed[...] = jnp.zeros(passed.shape, passed.dtype)
        kept[...] = jnp.zeros(kept.shape, kept.dtype)

    @pl.when(live_rows > 0)
    def _():
        own_rows = pl.ds(pl.multiple_of(row_start, GROUP), rows)
        for s in range(PHYS):
            for v in range(vectors):
                kept[0, s, v] = padded[slot, s, own_rows, v * LANES : v * LANES + cols]

        def mix(g, carry):
            here = pl.ds(pl.multiple_of(g * GROUP, GROUP), GROUP)
            for e, (low, high) in channel_slices.items():
                block = left[0, low:high, here, :].reshape((high - low) * GROUP, bond)
                block = jnp.concatenate([block, block], 0)
                total = jnp.dot(mixers[e][...], block, preferred_element_type=jnp.float32)
                at = offsets[(e,) + blocks[e][0]]
                n = mixers[e].shape[0] // GROUP
                mixed[at : at + n, here, :] = total.astype(mixed.dtype).reshape(n, GROUP, bond)
            return carry

        lax.fori_loop(0, live_rows // GROUP, mix, 0)
        chunks = live_rows // chunk

        for t in range(PHYS):
            if t == 0:
                right[:, :cols, :] = right_same[0]
            else:

                @pl.when(step < count - 1)
                def _():
                    right[:, :cols, :] = right_next[0]

                @pl.when(step == count - 1)
                def _():
                    pairs = channel_count // 2
                    right[:, :cols, :LANES] = right_last[:channel_count]
                    tails = right_last[channel_count:]
                    right[:pairs, :cols, LANES:] = tails[:, :, : bond - LANES]
                    right[pairs:, :cols, LANES:] = tails[:, :, bond - LANES :]

            def combine(r, carry):
                here = pl.ds(pl.multiple_of(r * chunk, chunk), chunk)
                for x, (low, high) in channel_slices.items():
                    n, total = high - low, None
                    for (e, tt, s, xx), at in offsets.items():
                        if (tt, xx) != (t, x):
                            continue
                        rows_of = mixed[at : at + n, here, :].reshape(n * chunk, bond)
                        term = jnp.dot(
                            rows_of, padded[slot - e, s], preferred_element_type=jnp.float32
                        )
                        total = term if total is None else total + term
                    total = total.astype(combined.dtype)
                    for i in range(n):
                        for v in range(vectors):
                            combined[v, here, (low + i) * LANES : (low + i + 1) * LANES] = total[
                                i * chunk : (i + 1) * chunk, v * LANES : (v + 1) * LANES
                            ]
                return carry

            lax.fori_loop(0, chunks, combine, 0)
            for n in range(1, rows // chunk + 1):

                @pl.when(chunks == n)
                def _(n=n):
                    m = n * chunk
                    total = jnp.dot(
                        combined[:, :m, :].reshape(vectors * m, channel_count * LANES),
                        right[...].reshape(channel_count * LANES, bond),
                        preferred_element_type=jnp.float32,
                    )
                    ids = lax.broadcasted_iota(jnp.int32, (m, cols), 1)
                    low_half = ids < info[slot + t]
                    high_half = ids + cols < info[slot + t]
                    for v in range(vectors):
                        piece = total[v * m : (v + 1) * m]
                        low_piece = jnp.where(low_half, piece[:, :cols], 0.0)
                        high_piece = jnp.where(high_half, piece[:, cols:], 0.0)
                        own = jnp.where(col_start == 0, low_piece, high_piece)
                        sent = jnp.where(col_start == 0, high_piece, low_piece)
                        out[0, t, v, :m, :] = own
                        passed[0, t, v, :m, :] = sent.astype(passed.dtype)
                        if m < rows:
                            rest = (rows - m, cols)
                            out[0, t, v, m:, :] = jnp.zeros(rest, out.dtype)
                            passed[0, t, v, m:, :] = jnp.zeros(rest, passed.dtype)


def applied_parts(info, source, left_env, right_env, right_last, mixers, vectors):
    slots, phys, bond, cells = source.shape
    count = left_env.shape[0]
    rows, cols = left_env.shape[2], right_env.shape[2]

    def whole(array):
        return pl.BlockSpec(array.shape, lambda q, info: (0,) * array.ndim)

    def result(q, info):
        return (q, 0, 0, 0, 0)

    block = (1, phys, vectors, rows, cols)
    full = (count, phys, vectors, rows, cols)
    grid_spec = pltpu.PrefetchScalarGridSpec(
        num_scalar_prefetch=1,
        grid=(count,),
        in_specs=[
            whole(source),
            pl.BlockSpec((1, channel_count, rows, bond), lambda q, info: (q, 0, 0, 0)),
            pl.BlockSpec((1, channel_count, cols, bond), lambda q, info: (q, 0, 0, 0)),
            pl.BlockSpec(
                (1, channel_count, cols, bond),
                lambda q, info: (jnp.minimum(q + 1, count - 1), 0, 0, 0),
            ),
            whole(right_last),
        ]
        + [whole(m) for m in mixers],
        out_specs=[pl.BlockSpec(block, result) for _ in range(3)],
        scratch_shapes=[
            pltpu.VMEM((slots, phys, bond, vectors * LANES), jnp.bfloat16),
            pltpu.VMEM((block_total, rows, bond), jnp.bfloat16),
            pltpu.VMEM((vectors, rows, channel_count * LANES), jnp.bfloat16),
            pltpu.VMEM((channel_count, LANES, bond), jnp.bfloat16),
        ],
    )
    return pl.pallas_call(
        functools.partial(apply_kernel, count, vectors),
        grid_spec=grid_spec,
        out_shape=[
            jax.ShapeDtypeStruct(full, jnp.float32),
            jax.ShapeDtypeStruct(full, jnp.bfloat16),
            jax.ShapeDtypeStruct(full, jnp.bfloat16),
        ],
        compiler_params=pltpu.CompilerParams(
            vmem_limit_bytes=38 * 1024 * 1024, dimension_semantics=("arbitrary",)
        ),
        cost_estimate=pl.CostEstimate(
            flops=5 * 10**9 * count, bytes_accessed=12 * 10**6, transcendentals=0
        ),
        name="apply_sectors",
    )(info, source, left_env, right_env, right_env, right_last, *mixers)


def ratio(top, bottom):
    return jnp.where(bottom > 0, top / jnp.where(bottom > 0, bottom, 1.0), 0.0)


def merged(slots):
    weights = [s[0] for s in slots]
    correlations = [s[1] for s in slots]
    squares = [s[2] for s in slots]
    weight, correlation, squared = sum(weights), sum(correlations), sum(squares)
    center = ratio(correlation, weight)
    for w, c in zip(weights, correlations):
        shift = ratio(c, w) - center
        squared = squared + shift * shift * w
    return weight, correlation, squared


def finish_kernel(
    vectors,
    own_ref,
    passed,
    kept_ref,
    out,
    scalars,
    value_of,
    kept,
    arrived,
    totals,
    near,
    far,
    own_sem,
    kept_sem,
    send_sem,
    recv_sem,
    near_send,
    near_recv,
    far_send,
    far_recv,
):
    nz, nx, nc = lax.axis_size("wide"), lax.axis_size("narrow"), lax.axis_size("rep")
    z, x, c = lax.axis_index("wide"), lax.axis_index("narrow"), lax.axis_index("rep")
    total = nx * nc
    place = x * nc + c
    blocks_here = arrived.shape[0]
    pieces = send_sem.shape[0]
    per_piece = blocks_here // pieces
    loads = []
    for k in range(pieces):
        here = pl.ds(k * per_piece, per_piece)
        loads.append(
            (
                pltpu.make_async_copy(own_ref.at[here], value_of.at[here], own_sem.at[k]),
                pltpu.make_async_copy(kept_ref.at[here], kept.at[here], kept_sem.at[k]),
            )
        )
        for one in loads[-1]:
            one.start()

    def near_id(d):
        target = lax.rem(place + d, total)
        return {"narrow": target // nc, "rep": lax.rem(target, nc)}

    def far_id(d):
        return {"wide": lax.rem(z + d, nz)}

    barrier = pltpu.get_barrier_semaphore()
    for d in range(1, total):
        pl.semaphore_signal(barrier, inc=1, device_id=near_id(d), device_id_type=MESH)
    for d in range(1, nz):
        pl.semaphore_signal(barrier, inc=1, device_id=far_id(d), device_id_type=MESH)
    pl.semaphore_wait(barrier, total + nz - 2)

    exchanges = []
    for k in range(pieces):
        here = pl.ds(k * per_piece, per_piece)
        exchanges.append(
            pltpu.make_async_remote_copy(
                src_ref=passed.at[here],
                dst_ref=arrived.at[here],
                send_sem=send_sem.at[k],
                recv_sem=recv_sem.at[k],
                device_id={"rep": 1 - c},
                device_id_type=MESH,
            )
        )
        exchanges[-1].start()

    rows, cols = arrived.shape[1:]
    totals[...] = jnp.zeros(totals.shape, jnp.float32)
    for k in range(pieces):
        for one in loads[k]:
            one.wait()
        exchanges[k].wait_recv()

        def first_pass(v, carry):
            weight, correlation = totals[0, v], totals[1, v]
            for i in range(per_piece // vectors):
                at = k * per_piece + i * vectors + v
                value = value_of[at] + arrived[at].astype(jnp.float32)
                value_of[at] = value
                state = kept[at].astype(jnp.float32)
                weight += state * state
                correlation += state * value
            totals[0, v] = weight
            totals[1, v] = correlation
            return carry

        lax.fori_loop(0, vectors, first_pass, 0)

    def reduced(sums):
        tile = jnp.zeros((8, cols), jnp.float32)
        line = lax.broadcasted_iota(jnp.int32, (8, cols), 0)
        for v, value in enumerate(sums):
            tile = jnp.where(line == v, jnp.sum(value, axis=0, keepdims=True), tile)
        return jnp.broadcast_to(jnp.sum(tile, axis=1, keepdims=True), (8, LANES))

    weight = reduced([totals[0, v] for v in range(vectors)])
    correlation = reduced([totals[1, v] for v in range(vectors)])
    center = ratio(correlation, weight)
    totals[0] = jnp.zeros(totals.shape[1:], jnp.float32)

    def second_pass(i, carry):
        for v in range(vectors):
            at = i * vectors + v
            rest = value_of[at] - center[v : v + 1, :cols] * kept[at].astype(jnp.float32)
            totals[0, v] += rest * rest
        return carry

    lax.fori_loop(0, blocks_here // vectors, second_pass, 0)
    squared = reduced([totals[0, v] for v in range(vectors)])
    near[place, 0] = weight
    near[place, 1] = correlation
    near[place, 2] = squared
    copies = [
        pltpu.make_async_remote_copy(
            src_ref=near.at[place],
            dst_ref=near.at[place],
            send_sem=near_send.at[d],
            recv_sem=near_recv.at[d],
            device_id=near_id(d),
            device_id_type=MESH,
        )
        for d in range(1, total)
    ]
    for one in copies:
        one.start()
    for one in copies:
        one.wait_recv()
    for i, value in enumerate(merged([near[j] for j in range(total)])):
        far[z, i] = value
    far_copies = [
        pltpu.make_async_remote_copy(
            src_ref=far.at[z],
            dst_ref=far.at[z],
            send_sem=far_send.at[d],
            recv_sem=far_recv.at[d],
            device_id=far_id(d),
            device_id_type=MESH,
        )
        for d in range(1, nz)
    ]
    for one in far_copies:
        one.start()
    for one in far_copies:
        one.wait_recv()
    weight, correlation, squared = merged([far[i] for i in range(nz)])
    alpha = correlation / weight
    beta = jnp.sqrt((squared + small_term) / weight)
    scalars[0] = alpha
    scalars[1] = beta
    scale = 1.0 / beta

    def last_pass(i, carry):
        for v in range(vectors):
            at = i * vectors + v
            rest = value_of[at] - alpha[v : v + 1, :cols] * kept[at].astype(jnp.float32)
            out[at] = (rest * scale[v : v + 1, :cols]).astype(out.dtype)
        return carry

    lax.fori_loop(0, blocks_here // vectors, last_pass, 0)
    for one in exchanges + copies + far_copies:
        one.wait_send()


def finished(own, passed, kept, vectors):
    blocks_here, rows, cols = own.shape
    near_count = lax.axis_size("narrow") * lax.axis_size("rep")
    far_count = lax.axis_size("wide")
    pieces = blocks_here // (PHYS * vectors)
    dma = pltpu.SemaphoreType.DMA
    return pl.pallas_call(
        functools.partial(finish_kernel, vectors),
        out_shape=[
            jax.ShapeDtypeStruct((blocks_here, rows, cols), jnp.bfloat16),
            jax.ShapeDtypeStruct((2, 8, LANES), jnp.float32),
        ],
        in_specs=[pl.BlockSpec(memory_space=pltpu.HBM)] * 3,
        out_specs=[pl.BlockSpec(memory_space=pltpu.VMEM)] * 2,
        scratch_shapes=[
            pltpu.VMEM((blocks_here, rows, cols), jnp.float32),
            pltpu.VMEM((blocks_here, rows, cols), jnp.bfloat16),
            pltpu.VMEM((blocks_here, rows, cols), jnp.bfloat16),
            pltpu.VMEM((2, vectors, rows, cols), jnp.float32),
            pltpu.VMEM((near_count, 3, 8, LANES), jnp.float32),
            pltpu.VMEM((far_count, 3, 8, LANES), jnp.float32),
            dma((pieces,)),
            dma((pieces,)),
            dma((pieces,)),
            dma((pieces,)),
            dma((near_count,)),
            dma((near_count,)),
            dma((far_count,)),
            dma((far_count,)),
        ],
        compiler_params=pltpu.CompilerParams(
            collective_id=1, has_side_effects=True, vmem_limit_bytes=14 * 1024 * 1024
        ),
        name="finish_step",
    )(own, passed, kept)


def body(state, left_env, right_env, mpo_tensor, sector_units, chosen):
    owned, phys, rows, vectors, cols = state.shape
    first_sector = lax.axis_index("wide") * owned
    row_start = lax.axis_index("narrow") * rows
    col_start = lax.axis_index("rep") * cols
    none = jnp.zeros((1,), jnp.int32)
    sizes = jnp.concatenate([none, sector_units * UNIT, none, none])
    info = jnp.concatenate(
        [
            lax.dynamic_slice_in_dim(sizes, first_sector, owned + 3),
            row_start[None],
            col_start[None],
            lax.dynamic_slice_in_dim(chosen, first_sector, owned),
        ]
    ).astype(jnp.int32)
    rule = jnp.transpose(mpo_tensor, (2, 3, 1, 0))
    source, following, *mixers = gathered(
        state.reshape(owned, phys, rows, vectors * cols), packed_lanes(right_env[0]), rule
    )
    parts = applied_parts(info, source, left_env, right_env, following, mixers, vectors)
    out, scalars = finished(
        *(part.reshape(owned * phys * vectors, rows, cols) for part in parts), vectors
    )
    next_state = out.reshape(owned, phys, vectors, rows, cols).transpose(0, 1, 3, 2, 4)
    return (next_state, scalars[0, :vectors, 0], scalars[1, :vectors, 0])


def solution(mesh):
    placed = (
        P(("groups", "wide"), None, "narrow", None, "rep"),
        P(("groups", "wide"), None, "narrow", None),
        P(("groups", "wide"), None, "rep", None),
        P(),
        P("groups"),
        P("groups"),
    )
    return jax.shard_map(
        body,
        mesh=mesh,
        in_specs=placed,
        out_specs=(P(("groups", "wide"), None, "narrow", None, "rep"), P("groups"), P("groups")),
        check_vma=False,
    )
```

```python
import functools
import jax
import jax.numpy as jnp
from jax import lax
from jax.experimental import pallas as pl
from jax.experimental.pallas import tpu as pltpu
from jax.sharding import PartitionSpec as P

UNIT = 32
PHYS = 2
LANES = 128
GROUP = 16
MESH = pl.DeviceIdType.MESH

small_term = 1e-06
channel_slices = {0: (0, 10), 1: (10, 17), -1: (17, 24)}
channel_count = 24
blocks = {
    0: ((0, 0, 0), (1, 1, 0), (1, 0, 1), (0, 1, -1)),
    1: ((0, 0, 1), (1, 1, 1), (0, 1, 0)),
    -1: ((0, 0, -1), (1, 1, -1), (1, 0, 0)),
}


def width(charge):
    low, high = channel_slices[charge]
    return high - low


def block_table():
    table, at = {}, 0
    for e, entries in blocks.items():
        for t, s, x in entries:
            table[(e, t, s, x)] = at
            at += width(x)
    return table, at


offsets, block_total = block_table()


def packed_lanes(block):
    half = block.shape[0] // 2
    rest = block[:, :, LANES:]
    return jnp.concatenate(
        [block[:, :, :LANES], jnp.concatenate([rest[:half], rest[half:]], 2)], 0
    )


def spread(rule, mixers):
    for e, (low, high) in channel_slices.items():
        n, depth = high - low, 2 * (high - low) * GROUP
        at = 0
        for t, s, x in blocks[e]:
            x_low, x_high = channel_slices[x]
            m = x_high - x_low
            exact = rule[t, s, x_low:x_high, low:high]
            coarse = exact.astype(jnp.bfloat16)
            rest = (exact - coarse.astype(jnp.float32)).astype(jnp.bfloat16)
            row = lax.broadcasted_iota(jnp.int32, (m * GROUP, m), 0) // GROUP
            up = jnp.where(row == lax.broadcasted_iota(jnp.int32, (m * GROUP, m), 1), 1.0, 0.0)
            up = up.astype(jnp.bfloat16)
            col = lax.broadcasted_iota(jnp.int32, (n, depth), 1) // GROUP
            line = lax.broadcasted_iota(jnp.int32, (n, depth), 0)
            total = None
            for part, start in ((coarse, 0), (rest, n)):
                side = jnp.where(col == line + start, 1.0, 0.0).astype(jnp.bfloat16)
                tall = jnp.dot(up, part, preferred_element_type=jnp.float32).astype(jnp.bfloat16)
                term = jnp.dot(tall, side, preferred_element_type=jnp.float32)
                total = term if total is None else total + term
            shape = (m * GROUP, depth)
            same = lax.broadcasted_iota(jnp.int32, shape, 0) % GROUP == (
                lax.broadcasted_iota(jnp.int32, shape, 1) % GROUP
            )
            mixers[e][at : at + m * GROUP, :] = jnp.where(same, total, 0.0).astype(jnp.bfloat16)
            at += m * GROUP


def gather_kernel(
    state_ref,
    packed_ref,
    rule,
    out_ref,
    following_ref,
    mix_zero,
    mix_up,
    mix_down,
    local_sem,
    halo_send,
    halo_recv,
    cross_send,
    cross_recv,
    right_send,
    right_recv,
):
    nz, nx = lax.axis_size("wide"), lax.axis_size("narrow")
    z, x = lax.axis_index("wide"), lax.axis_index("narrow")
    owned, _, rows, _ = state_ref.shape
    mine = pl.ds(pl.multiple_of(x * rows, GROUP), rows)
    below, above = z > 0, z < nz - 1

    def other(dx):
        return lax.rem(x + dx, nx)

    barrier = pltpu.get_barrier_semaphore()
    for dx in range(1, nx):
        pl.semaphore_signal(barrier, inc=1, device_id={"narrow": other(dx)}, device_id_type=MESH)

    @pl.when(above)
    def _():
        pl.semaphore_signal(barrier, inc=1, device_id={"wide": z + 1}, device_id_type=MESH)

    @pl.when(below)
    def _():
        pl.semaphore_signal(barrier, inc=1, device_id={"wide": z - 1}, device_id_type=MESH)

    sides = jnp.where(below, 1, 0) + jnp.where(above, 1, 0)
    pl.semaphore_wait(barrier, nx - 1 + sides)

    def along(kind, step, source, target):
        return pltpu.make_async_remote_copy(
            src_ref=source,
            dst_ref=target,
            send_sem=halo_send.at[kind],
            recv_sem=halo_recv.at[kind],
            device_id={"wide": z + step},
            device_id_type=MESH,
        )

    def across(kind, dx, source, target):
        return pltpu.make_async_remote_copy(
            src_ref=source,
            dst_ref=target,
            send_sem=cross_send.at[kind, dx],
            recv_sem=cross_recv.at[kind, dx],
            device_id={"narrow": other(dx)},
            device_id_type=MESH,
        )

    first, last = out_ref.at[0, :, mine], out_ref.at[owned + 1, :, mine]
    middle = out_ref.at[pl.ds(1, owned), :, mine]
    up = along(0, 1, state_ref.at[owned - 1], first)
    down = along(1, -1, state_ref.at[0], last)
    right = pltpu.make_async_remote_copy(
        src_ref=packed_ref,
        dst_ref=following_ref,
        send_sem=right_send,
        recv_sem=right_recv,
        device_id={"wide": z - 1},
        device_id_type=MESH,
    )
    own = [across(0, dx, state_ref, middle) for dx in range(1, nx)]
    firsts = [across(1, dx, first, first) for dx in range(1, nx)]
    lasts = [across(2, dx, last, last) for dx in range(1, nx)]
    keep = pltpu.make_async_copy(state_ref, middle, local_sem)

    @pl.when(below)
    def _():
        down.start()
        right.start()

    @pl.when(above)
    def _():
        up.start()

    for one in own:
        one.start()
    keep.start()

    @pl.when(below)
    def _():
        up.wait_recv()
        for one in firsts:
            one.start()

    @pl.when(above)
    def _():
        down.wait_recv()
        for one in lasts:
            one.start()

    spread(rule, {0: mix_zero, 1: mix_up, -1: mix_down})

    keep.wait()
    for one in own:
        one.wait_send()
        one.wait_recv()

    @pl.when(below)
    def _():
        for one in firsts:
            one.wait_send()
            one.wait_recv()
        down.wait_send()
        right.wait_send()

    @pl.when(above)
    def _():
        up.wait_send()
        for one in lasts:
            one.wait_send()
            one.wait_recv()
        right.wait_recv()


def mixer_shape(e):
    return (GROUP * sum(width(x) for _, _, x in blocks[e]), 2 * GROUP * width(e))


def gathered(state, packed, rule):
    owned, phys, rows, cells = state.shape
    nx = lax.axis_size("narrow")
    hbm = pl.BlockSpec(memory_space=pltpu.HBM)
    vmem = pl.BlockSpec(memory_space=pltpu.VMEM)
    dma = pltpu.SemaphoreType.DMA
    return pl.pallas_call(
        gather_kernel,
        out_shape=[
            jax.ShapeDtypeStruct((owned + 2, phys, rows * nx, cells), state.dtype),
            jax.ShapeDtypeStruct(packed.shape, packed.dtype),
        ]
        + [jax.ShapeDtypeStruct(mixer_shape(e), jnp.bfloat16) for e in channel_slices],
        in_specs=[hbm, hbm, vmem],
        out_specs=[hbm, hbm, vmem, vmem, vmem],
        scratch_shapes=[dma, dma((2,)), dma((2,)), dma((3, nx)), dma((3, nx)), dma, dma],
        compiler_params=pltpu.CompilerParams(
            collective_id=0, has_side_effects=True, vmem_limit_bytes=12 * 1024 * 1024
        ),
        cost_estimate=pl.CostEstimate(
            flops=10**8, bytes_accessed=60 * 10**6, transcendentals=0
        ),
        name="gather_state",
    )(state, packed, rule)


def apply_kernel(
    count,
    vectors,
    info,
    source,
    left,
    right_same,
    right_next,
    right_last,
    mix_zero,
    mix_up,
    mix_down,
    out,
    passed,
    kept,
    padded,
    mixed,
    combined,
    right,
):
    step = pl.program_id(0)
    rows, bond = left.shape[2], left.shape[3]
    cols = right_same.shape[2]
    chunk = 32 if rows % 32 == 0 else GROUP
    slots = padded.shape[0]
    slot = step + 1
    base = slots + 1
    row_start, col_start = info[base], info[base + 1]
    chosen = info[base + 2 + step]
    mixers = {0: mix_zero, 1: mix_up, -1: mix_down}

    @pl.when(step == 0)
    def _():
        right[:, cols:, :] = jnp.zeros((channel_count, LANES - cols, bond), right.dtype)
        padded[...] = jnp.zeros(padded.shape, padded.dtype)
        col_ids = lax.broadcasted_iota(jnp.int32, (UNIT, cols), 1) + col_start

        def fill(j, carry):
            def fill_unit(u, carry):
                here = pl.ds(pl.multiple_of(u * UNIT, UNIT), UNIT)
                for s in range(PHYS):
                    live = col_ids < info[j + s]
                    for v in range(vectors):
                        part = source[j, s, here, v * cols : (v + 1) * cols].astype(jnp.float32)
                        part = jnp.where(live, part, 0.0).astype(padded.dtype)
                        padded[j, s, here, v * LANES : v * LANES + cols] = part
                return carry

            return lax.fori_loop(0, info[j] // UNIT, fill_unit, carry)

        lax.fori_loop(0, slots, fill, 0)

    live_rows = jnp.clip(info[slot] - row_start, 0, rows) * jnp.where(chosen > 0, 1, 0)

    @pl.when(live_rows == 0)
    def _():
        out[...] = jnp.zeros(out.shape, out.dtype)
        passed[...] = jnp.zeros(passed.shape, passed.dtype)
        kept[...] = jnp.zeros(kept.shape, kept.dtype)

    @pl.when(live_rows > 0)
    def _():
        own_rows = pl.ds(pl.multiple_of(row_start, GROUP), rows)
        for s in range(PHYS):
            for v in range(vectors):
                kept[0, s, v] = padded[slot, s, own_rows, v * LANES : v * LANES + cols]

        def mix(g, carry):
            here = pl.ds(pl.multiple_of(g * GROUP, GROUP), GROUP)
            for e, (low, high) in channel_slices.items():
                block = left[0, low:high, here, :].reshape((high - low) * GROUP, bond)
                block = jnp.concatenate([block, block], 0)
                total = jnp.dot(mixers[e][...], block, preferred_element_type=jnp.float32)
                at = offsets[(e,) + blocks[e][0]]
                n = mixers[e].shape[0] // GROUP
                mixed[at : at + n, here, :] = total.astype(mixed.dtype).reshape(n, GROUP, bond)
            return carry

        lax.fori_loop(0, live_rows // GROUP, mix, 0)
        chunks = live_rows // chunk

        for t in range(PHYS):
            if t == 0:
                right[:, :cols, :] = right_same[0]
            else:

                @pl.when(step < count - 1)
                def _():
                    right[:, :cols, :] = right_next[0]

                @pl.when(step == count - 1)
                def _():
                    pairs = channel_count // 2
                    right[:, :cols, :LANES] = right_last[:channel_count]
                    tails = right_last[channel_count:]
                    right[:pairs, :cols, LANES:] = tails[:, :, : bond - LANES]
                    right[pairs:, :cols, LANES:] = tails[:, :, bond - LANES :]

            def combine(packed, r, carry):
                here = pl.ds(pl.multiple_of(r * chunk, chunk), chunk)
                for x, (low, high) in channel_slices.items():
                    n = high - low
                    terms = [
                        (at, slot - e, s)
                        for (e, tt, s, xx), at in offsets.items()
                        if (tt, xx) == (t, x)
                    ]
                    if packed and len(terms) == 2:
                        sides = [mixed[at : at + n, here, :LANES] for at, _, _ in terms]
                        total = jnp.dot(
                            jnp.concatenate(sides, 2).reshape(n * chunk, 2 * LANES),
                            jnp.concatenate([padded[j, s, :LANES] for _, j, s in terms], 0),
                            preferred_element_type=jnp.float32,
                        )
                    else:
                        total = None
                        for at, j, s in terms:
                            rows_of = mixed[at : at + n, here, :].reshape(n * chunk, bond)
                            term = jnp.dot(
                                rows_of, padded[j, s], preferred_element_type=jnp.float32
                            )
                            total = term if total is None else total + term
                    total = total.astype(combined.dtype)
                    for i in range(n):
                        for v in range(vectors):
                            combined[v, here, (low + i) * LANES : (low + i + 1) * LANES] = total[
                                i * chunk : (i + 1) * chunk, v * LANES : (v + 1) * LANES
                            ]
                return carry

            largest = jnp.maximum(jnp.maximum(info[slot - 1], info[slot]), info[slot + 1])
            fits = largest <= LANES
            lax.fori_loop(0, jnp.where(fits, chunks, 0), functools.partial(combine, True), 0)
            lax.fori_loop(0, jnp.where(fits, 0, chunks), functools.partial(combine, False), 0)
            for n in range(1, rows // chunk + 1):

                @pl.when(chunks == n)
                def _(n=n):
                    m = n * chunk
                    total = jnp.dot(
                        combined[:, :m, :].reshape(vectors * m, channel_count * LANES),
                        right[...].reshape(channel_count * LANES, bond),
                        preferred_element_type=jnp.float32,
                    )
                    ids = lax.broadcasted_iota(jnp.int32, (m, cols), 1)
                    low_half = ids < info[slot + t]
                    high_half = ids + cols < info[slot + t]
                    for v in range(vectors):
                        piece = total[v * m : (v + 1) * m]
                        low_piece = jnp.where(low_half, piece[:, :cols], 0.0)
                        high_piece = jnp.where(high_half, piece[:, cols:], 0.0)
                        own = jnp.where(col_start == 0, low_piece, high_piece)
                        sent = jnp.where(col_start == 0, high_piece, low_piece)
                        out[0, t, v, :m, :] = own
                        passed[0, t, v, :m, :] = sent.astype(passed.dtype)
                        if m < rows:
                            rest = (rows - m, cols)
                            out[0, t, v, m:, :] = jnp.zeros(rest, out.dtype)
                            passed[0, t, v, m:, :] = jnp.zeros(rest, passed.dtype)


def applied_parts(info, source, left_env, right_env, right_last, mixers, vectors):
    slots, phys, bond, cells = source.shape
    count = left_env.shape[0]
    rows, cols = left_env.shape[2], right_env.shape[2]

    def whole(array):
        return pl.BlockSpec(array.shape, lambda q, info: (0,) * array.ndim)

    def result(q, info):
        return (q, 0, 0, 0, 0)

    block = (1, phys, vectors, rows, cols)
    full = (count, phys, vectors, rows, cols)
    grid_spec = pltpu.PrefetchScalarGridSpec(
        num_scalar_prefetch=1,
        grid=(count,),
        in_specs=[
            whole(source),
            pl.BlockSpec((1, channel_count, rows, bond), lambda q, info: (q, 0, 0, 0)),
            pl.BlockSpec((1, channel_count, cols, bond), lambda q, info: (q, 0, 0, 0)),
            pl.BlockSpec(
                (1, channel_count, cols, bond),
                lambda q, info: (jnp.minimum(q + 1, count - 1), 0, 0, 0),
            ),
            whole(right_last),
        ]
        + [whole(m) for m in mixers],
        out_specs=[pl.BlockSpec(block, result) for _ in range(3)],
        scratch_shapes=[
            pltpu.VMEM((slots, phys, bond, vectors * LANES), jnp.bfloat16),
            pltpu.VMEM((block_total, rows, bond), jnp.bfloat16),
            pltpu.VMEM((vectors, rows, channel_count * LANES), jnp.bfloat16),
            pltpu.VMEM((channel_count, LANES, bond), jnp.bfloat16),
        ],
    )
    return pl.pallas_call(
        functools.partial(apply_kernel, count, vectors),
        grid_spec=grid_spec,
        out_shape=[
            jax.ShapeDtypeStruct(full, jnp.float32),
            jax.ShapeDtypeStruct(full, jnp.bfloat16),
            jax.ShapeDtypeStruct(full, jnp.bfloat16),
        ],
        compiler_params=pltpu.CompilerParams(
            vmem_limit_bytes=38 * 1024 * 1024, dimension_semantics=("arbitrary",)
        ),
        cost_estimate=pl.CostEstimate(
            flops=5 * 10**9 * count, bytes_accessed=12 * 10**6, transcendentals=0
        ),
        name="apply_sectors",
    )(info, source, left_env, right_env, right_env, right_last, *mixers)


def ratio(top, bottom):
    return jnp.where(bottom > 0, top / jnp.where(bottom > 0, bottom, 1.0), 0.0)


def merged(slots):
    weights = [s[0] for s in slots]
    correlations = [s[1] for s in slots]
    squares = [s[2] for s in slots]
    weight, correlation, squared = sum(weights), sum(correlations), sum(squares)
    center = ratio(correlation, weight)
    for w, c in zip(weights, correlations):
        shift = ratio(c, w) - center
        squared = squared + shift * shift * w
    return weight, correlation, squared


def finish_kernel(
    vectors,
    own_ref,
    passed,
    kept_ref,
    out,
    scalars,
    value_of,
    kept,
    arrived,
    totals,
    near,
    far,
    own_sem,
    kept_sem,
    send_sem,
    recv_sem,
    near_send,
    near_recv,
    far_send,
    far_recv,
):
    nz, nx, nc = lax.axis_size("wide"), lax.axis_size("narrow"), lax.axis_size("rep")
    z, x, c = lax.axis_index("wide"), lax.axis_index("narrow"), lax.axis_index("rep")
    total = nx * nc
    place = x * nc + c
    blocks_here = arrived.shape[0]
    pieces = send_sem.shape[0]
    per_piece = blocks_here // pieces
    loads = []
    for k in range(pieces):
        here = pl.ds(k * per_piece, per_piece)
        loads.append(
            (
                pltpu.make_async_copy(own_ref.at[here], value_of.at[here], own_sem.at[k]),
                pltpu.make_async_copy(kept_ref.at[here], kept.at[here], kept_sem.at[k]),
            )
        )
        for one in loads[-1]:
            one.start()

    def near_id(d):
        target = lax.rem(place + d, total)
        return {"narrow": target // nc, "rep": lax.rem(target, nc)}

    def far_id(d):
        return {"wide": lax.rem(z + d, nz)}

    barrier = pltpu.get_barrier_semaphore()
    for d in range(1, total):
        pl.semaphore_signal(barrier, inc=1, device_id=near_id(d), device_id_type=MESH)
    for d in range(1, nz):
        pl.semaphore_signal(barrier, inc=1, device_id=far_id(d), device_id_type=MESH)
    pl.semaphore_wait(barrier, total + nz - 2)

    exchanges = []
    for k in range(pieces):
        here = pl.ds(k * per_piece, per_piece)
        exchanges.append(
            pltpu.make_async_remote_copy(
                src_ref=passed.at[here],
                dst_ref=arrived.at[here],
                send_sem=send_sem.at[k],
                recv_sem=recv_sem.at[k],
                device_id={"rep": 1 - c},
                device_id_type=MESH,
            )
        )
        exchanges[-1].start()

    rows, cols = arrived.shape[1:]
    totals[...] = jnp.zeros(totals.shape, jnp.float32)
    for k in range(pieces):
        for one in loads[k]:
            one.wait()
        exchanges[k].wait_recv()

        def first_pass(v, carry):
            weight, correlation = totals[0, v], totals[1, v]
            for i in range(per_piece // vectors):
                at = k * per_piece + i * vectors + v
                value = value_of[at] + arrived[at].astype(jnp.float32)
                value_of[at] = value
                state = kept[at].astype(jnp.float32)
                weight += state * state
                correlation += state * value
            totals[0, v] = weight
            totals[1, v] = correlation
            return carry

        lax.fori_loop(0, vectors, first_pass, 0)

    def reduced(sums):
        tile = jnp.zeros((8, cols), jnp.float32)
        line = lax.broadcasted_iota(jnp.int32, (8, cols), 0)
        for v, value in enumerate(sums):
            tile = jnp.where(line == v, jnp.sum(value, axis=0, keepdims=True), tile)
        return jnp.broadcast_to(jnp.sum(tile, axis=1, keepdims=True), (8, LANES))

    weight = reduced([totals[0, v] for v in range(vectors)])
    correlation = reduced([totals[1, v] for v in range(vectors)])
    center = ratio(correlation, weight)
    totals[0] = jnp.zeros(totals.shape[1:], jnp.float32)

    def second_pass(i, carry):
        for v in range(vectors):
            at = i * vectors + v
            rest = value_of[at] - center[v : v + 1, :cols] * kept[at].astype(jnp.float32)
            totals[0, v] += rest * rest
        return carry

    lax.fori_loop(0, blocks_here // vectors, second_pass, 0)
    squared = reduced([totals[0, v] for v in range(vectors)])
    near[place, 0] = weight
    near[place, 1] = correlation
    near[place, 2] = squared
    copies = [
        pltpu.make_async_remote_copy(
            src_ref=near.at[place],
            dst_ref=near.at[place],
            send_sem=near_send.at[d],
            recv_sem=near_recv.at[d],
            device_id=near_id(d),
            device_id_type=MESH,
        )
        for d in range(1, total)
    ]
    for one in copies:
        one.start()
    for one in copies:
        one.wait_recv()
    for i, value in enumerate(merged([near[j] for j in range(total)])):
        far[z, i] = value
    far_copies = [
        pltpu.make_async_remote_copy(
            src_ref=far.at[z],
            dst_ref=far.at[z],
            send_sem=far_send.at[d],
            recv_sem=far_recv.at[d],
            device_id=far_id(d),
            device_id_type=MESH,
        )
        for d in range(1, nz)
    ]
    for one in far_copies:
        one.start()
    for one in far_copies:
        one.wait_recv()
    weight, correlation, squared = merged([far[i] for i in range(nz)])
    alpha = correlation / weight
    beta = jnp.sqrt((squared + small_term) / weight)
    scalars[0] = alpha
    scalars[1] = beta
    scale = 1.0 / beta

    def last_pass(i, carry):
        for v in range(vectors):
            at = i * vectors + v
            rest = value_of[at] - alpha[v : v + 1, :cols] * kept[at].astype(jnp.float32)
            out[at] = (rest * scale[v : v + 1, :cols]).astype(out.dtype)
        return carry

    lax.fori_loop(0, blocks_here // vectors, last_pass, 0)
    for one in exchanges + copies + far_copies:
        one.wait_send()


def finished(own, passed, kept, vectors):
    blocks_here, rows, cols = own.shape
    near_count = lax.axis_size("narrow") * lax.axis_size("rep")
    far_count = lax.axis_size("wide")
    pieces = blocks_here // (PHYS * vectors)
    dma = pltpu.SemaphoreType.DMA
    return pl.pallas_call(
        functools.partial(finish_kernel, vectors),
        out_shape=[
            jax.ShapeDtypeStruct((blocks_here, rows, cols), jnp.bfloat16),
            jax.ShapeDtypeStruct((2, 8, LANES), jnp.float32),
        ],
        in_specs=[pl.BlockSpec(memory_space=pltpu.HBM)] * 3,
        out_specs=[pl.BlockSpec(memory_space=pltpu.VMEM)] * 2,
        scratch_shapes=[
            pltpu.VMEM((blocks_here, rows, cols), jnp.float32),
            pltpu.VMEM((blocks_here, rows, cols), jnp.bfloat16),
            pltpu.VMEM((blocks_here, rows, cols), jnp.bfloat16),
            pltpu.VMEM((2, vectors, rows, cols), jnp.float32),
            pltpu.VMEM((near_count, 3, 8, LANES), jnp.float32),
            pltpu.VMEM((far_count, 3, 8, LANES), jnp.float32),
            dma((pieces,)),
            dma((pieces,)),
            dma((pieces,)),
            dma((pieces,)),
            dma((near_count,)),
            dma((near_count,)),
            dma((far_count,)),
            dma((far_count,)),
        ],
        compiler_params=pltpu.CompilerParams(
            collective_id=1, has_side_effects=True, vmem_limit_bytes=14 * 1024 * 1024
        ),
        name="finish_step",
    )(own, passed, kept)


def body(state, left_env, right_env, mpo_tensor, sector_units, chosen):
    owned, phys, rows, vectors, cols = state.shape
    first_sector = lax.axis_index("wide") * owned
    row_start = lax.axis_index("narrow") * rows
    col_start = lax.axis_index("rep") * cols
    none = jnp.zeros((1,), jnp.int32)
    sizes = jnp.concatenate([none, sector_units * UNIT, none, none])
    info = jnp.concatenate(
        [
            lax.dynamic_slice_in_dim(sizes, first_sector, owned + 3),
            row_start[None],
            col_start[None],
            lax.dynamic_slice_in_dim(chosen, first_sector, owned),
        ]
    ).astype(jnp.int32)
    rule = jnp.transpose(mpo_tensor, (2, 3, 1, 0))
    source, following, *mixers = gathered(
        state.reshape(owned, phys, rows, vectors * cols), packed_lanes(right_env[0]), rule
    )
    parts = applied_parts(info, source, left_env, right_env, following, mixers, vectors)
    out, scalars = finished(
        *(part.reshape(owned * phys * vectors, rows, cols) for part in parts), vectors
    )
    next_state = out.reshape(owned, phys, vectors, rows, cols).transpose(0, 1, 3, 2, 4)
    return (next_state, scalars[0, :vectors, 0], scalars[1, :vectors, 0])


def solution(mesh):
    placed = (
        P(("groups", "wide"), None, "narrow", None, "rep"),
        P(("groups", "wide"), None, "narrow", None),
        P(("groups", "wide"), None, "rep", None),
        P(),
        P("groups"),
        P("groups"),
    )
    return jax.shard_map(
        body,
        mesh=mesh,
        in_specs=placed,
        out_specs=(P(("groups", "wide"), None, "narrow", None, "rep"), P("groups"), P("groups")),
        check_vma=False,
    )
```
